128 devices in a mesh: dp: 4 (over x_hi, core), tensor: 32 (over y, z, x_lo).
Axes of the slice: x: 4 (x_hi: 2, x_lo: 2; x = x_hi * 2 + x_lo), y: 4, z: 4, core: 2. Of those that a mesh axis runs over, the one named last changes fastest.
Arguments:
- hidden_in: bfloat16 [4096, 8192], P('dp'), may hold values from -6 to 6
- attn_gain: float32 [8192], replicated, may hold values from 0.1 to 1.9
- seg_ids: int32 [4096], P('dp'), may hold values from 0 to 15, never falling along the last dimension, each value on 1 to 512 neighbouring positions
- w_query: bfloat16 [8192, 8192], P(None, 'tensor'), may hold values from -0.0625 to 0.0625
- w_key: bfloat16 [8192, 1024], P(None, 'tensor'), may hold values from -0.0625 to 0.0625
- w_value: bfloat16 [8192, 1024], P(None, 'tensor'), may hold values from -0.0625 to 0.0625
- w_down: bfloat16 [8192, 1024], P('tensor'), may hold values from -0.1875 to 0.1875
- prev_side: bfloat16 [4096, 1024], P(('dp', 'tensor')), may hold values from -6 to 6
- gate_logit: float32 [1024], replicated, may hold values from -2 to 2
- side_gain: float32 [1024], replicated, may hold values from 0.5 to 1.5
- w_in: bfloat16 [1024, 1792], P('tensor'), may hold values from -0.1875 to 0.1875
- w_out: bfloat16 [1792, 1024], P('tensor'), may hold values from -0.125 to 0.125
- d_out: bfloat16 [4096, 1024], P(('dp', 'tensor')), may hold values from -6 to 6
Outputs:
- side_out: bfloat16 [4096, 1024], P(('dp', 'tensor'))
- d_prev: bfloat16 [4096, 1024], P(('dp', 'tensor'))
- g_down: float32 [8192, 1024], P('tensor')
- g_in: float32 [1024, 1792], P('tensor')
- g_out: float32 [1792, 1024], P('tensor')
- g_gain: float32 [1024], P('tensor')
- g_gate: float32 [1024], P('tensor')
The draws below stay inside these ranges and needn't reach their ends.
Inputs may be any that keep to these rules, and one draw needn't show every extreme that they name: `seg_ids`: segment numbers never fall along the tokens; each document spans at most 512 tokens and one spans exactly that many.
All inputs are finite; a program needn't handle non-finite values.
Results may differ from the reference program's by a relative error of at most 0.022.
Values may be sent and summed in bfloat16 or wider, within the bound.
A program may use at most 128 MiB of HBM per device.

```python
import math
import jax
import jax.numpy as jnp
import numpy as np
from jax import lax

D = 8192
HEADS = 64
KV = 8
HD = 128
SIDE = 1024
SFF = 1792
TOK_GRP = 1024
TOKENS = 4096
N_DP = 4


def steps_of(key, dims, shards, least, largest):
    def one(axis_at, parts):
        heights = jax.random.uniform(jax.random.fold_in(jax.random.fold_in(key, 6), axis_at), (parts,), jnp.float32, least / len(shards), largest / len(shards))
        return jnp.repeat(jnp.exp(heights), dims[axis_at] // parts).reshape((-1,) + (1,) * (len(dims) - axis_at - 1))

    factor_of = one(*shards[0])
    for cut in shards[1:]:
        factor_of = factor_of * one(*cut)
    return factor_of


def profile(amount, total, bound, slope):
    loads = [(1 << 20) // math.isqrt(rank ** slope) + 1 for rank in range(2, amount + 1)]
    surplus, given = total - bound - (amount - 1), [1] * (amount - 1)
    while surplus > 0:
        candidates = [i for i in range(amount - 1) if given[i] < bound]
        pool, remaining = sum([loads[i] for i in candidates]), surplus
        for i in candidates:
            extra = min(bound - given[i], max(1, remaining * loads[i] // pool), surplus)
            given[i] = given[i] + extra
            surplus = surplus - extra
    return np.array([bound] + given)


def ragged(key, number_of, total, most, skew):
    if number_of == 2:
        one = jax.random.randint(key, (), max(1, total - most), min(most, total - 1) + 1)
        return jnp.stack([one, total - one])
    lengths = jnp.asarray(profile(number_of, total, most, skew), jnp.int32)
    pairs = (number_of - 1) // 2
    source_of, receiver = lengths[1:1 + 2 * pairs:2], lengths[2:2 + 2 * pairs:2]
    slack = jnp.minimum(source_of - 1, most - receiver)
    shifted = jax.random.randint(jax.random.fold_in(key, 1), (pairs,), 0, 1 << 20) % (slack + 1)
    lengths = lengths.at[1:1 + 2 * pairs:2].set(source_of - shifted).at[2:2 + 2 * pairs:2].set(receiver + shifted)
    return lengths[jax.random.permutation(jax.random.fold_in(key, 2), number_of)]


def scatter_about(key, dims, width, most, split=(), kind=jnp.bfloat16):
    values = jax.random.normal(key, dims, jnp.float32) * width
    if len(split) > 0:
        values = steps_of(key, dims, split, -0.22, 0.18) * values
    return jnp.clip(values, min=-most, max=most).astype(kind)


def setup_inputs(seed: int = 0) -> dict:
    key_of = jax.random.split(jax.random.key(seed), 14)
    return {
        "hidden_in": scatter_about(key_of[0], (TOKENS, D), 1.0, 6.0, ((0, 4),)),
        "attn_gain": jnp.clip(1.0 + 0.18 * jax.random.normal(key_of[1], (D,), jnp.float32), 0.1, 1.9),
        "seg_ids": jnp.searchsorted(jnp.cumsum(ragged(key_of[2], 4 * N_DP, TOKENS, TOK_GRP // 2, 0)), jnp.arange(TOKENS), side="right").astype(jnp.int32),
        "w_query": scatter_about(key_of[3], (D, HEADS * HD), D ** -0.5, 0.0625, ((1, 32),)),
        "w_key": scatter_about(key_of[4], (D, KV * HD), D ** -0.5, 0.0625, ((1, 32),)),
        "w_value": scatter_about(key_of[5], (D, KV * HD), D ** -0.5, 0.0625, ((1, 32),)),
        "w_down": scatter_about(key_of[6], (HEADS * HD, SIDE), (D // 8) ** -0.5, 0.1875, ((0, 32),)),
        "prev_side": scatter_about(key_of[7], (TOKENS, SIDE), 1.0, 6.0, ((0, 128),)),
        "gate_logit": jnp.clip(jax.random.uniform(key_of[8], (SIDE,), jnp.float32, -2.0, 2.0), -2.0, 2.0),
        "side_gain": jnp.clip(1.0 + 0.1 * jax.random.normal(key_of[9], (SIDE,), jnp.float32), 0.5, 1.5),
        "w_in": scatter_about(key_of[10], (SIDE, SFF), SIDE ** -0.5, 0.1875, ((0, 32),)),
        "w_out": scatter_about(key_of[11], (SFF, SIDE), SFF ** -0.5, 0.125, ((0, 32),)),
        "d_out": scatter_about(key_of[12], (TOKENS, SIDE), 1.0, 6.0, ((0, 128),)),
    }


def positions(seg):
    count = seg.shape[0]
    idx = jnp.arange(count, dtype=jnp.int32)
    change = jnp.concatenate([jnp.ones((1,), dtype=bool), seg[1:] != seg[:-1]])
    start = lax.cummax(jnp.where(change, idx, jnp.zeros_like(idx)), axis=0)
    return (idx - start).astype(jnp.float32)

def rotate(vals, pos):
    half = vals.shape[-1] // 2
    freqs = 10000.0 ** (-jnp.arange(half, dtype=jnp.float32) * 2.0 / vals.shape[-1])
    angle = pos[:, None] * freqs[None, :]
    cosine = jnp.cos(angle)[:, None, :]
    sine = jnp.sin(angle)[:, None, :]
    first = vals[..., :half]
    second = vals[..., half:]
    return jnp.concatenate([first * cosine - second * sine, second * cosine + first * sine], axis=-1)

def group_context(inputs):
    xgrp, seg, attn_gain, w_query, w_key, w_value = inputs
    count = xgrp.shape[0]
    xf = xgrp.astype(jnp.float32)
    scale_rms = lax.rsqrt(lax.optimization_barrier(jnp.mean(xf * xf, axis=-1, keepdims=True)) + 1e-05)
    normed = (xf * scale_rms * attn_gain).astype(jnp.bfloat16)
    query = jnp.dot(normed, w_query, preferred_element_type=jnp.float32)
    key = jnp.dot(normed, w_key, preferred_element_type=jnp.float32).astype(jnp.bfloat16)
    value = jnp.dot(normed, w_value, preferred_element_type=jnp.float32).astype(jnp.bfloat16)
    pos = positions(seg)
    q_rot = rotate(query.reshape(count, HEADS, HD), pos).astype(jnp.bfloat16)
    k_rot = rotate(key.astype(jnp.float32).reshape(count, KV, HD), pos).astype(jnp.bfloat16)
    vals = value.reshape(count, KV, HD)
    group = HEADS // KV
    idx = jnp.arange(count, dtype=jnp.int32)
    allowed = (idx[None, :] <= idx[:, None]) & (seg[None, :] == seg[:, None])
    q_split = q_rot.reshape(count, KV, group, HD).transpose(1, 0, 2, 3)
    k_split = k_rot.transpose(1, 0, 2)
    v_split = vals.transpose(1, 0, 2)

    def one_head(pieces):
        qh, kh, vh = pieces
        scores = jnp.einsum('tgd,sd->gts', qh.astype(jnp.float32), kh.astype(jnp.float32)) / jnp.sqrt(jnp.float32(HD))
        expo = jnp.where(allowed[None], jnp.exp(scores), jnp.float32(0.0))
        probs = (expo / lax.optimization_barrier(jnp.sum(expo, axis=-1, keepdims=True))).astype(jnp.bfloat16)
        return jnp.einsum('gts,sd->tgd', probs.astype(jnp.float32), vh.astype(jnp.float32)).astype(jnp.bfloat16)
    ctx = lax.map(one_head, (q_split, k_split, v_split))
    return ctx.transpose(1, 0, 2, 3).reshape(count, HEADS * HD)

def reference(hidden_in, attn_gain, seg_ids, w_query, w_key, w_value, w_down, prev_side, gate_logit, side_gain, w_in, w_out, d_out):
    groups = hidden_in.shape[0] // TOK_GRP
    xgrp = hidden_in.reshape(groups, TOK_GRP, D)
    sgrp = seg_ids.reshape(groups, TOK_GRP)
    ctx = lax.map(lambda pair: group_context((pair[0], pair[1], attn_gain, w_query, w_key, w_value)), (xgrp, sgrp))
    ctx = ctx.reshape(groups * TOK_GRP, HEADS * HD)
    down = jnp.dot(ctx, w_down, preferred_element_type=jnp.float32)
    gate = jax.nn.sigmoid(gate_logit)
    prev = prev_side.astype(jnp.float32)
    mix = gate * down + (1.0 - gate) * prev
    rnorm = lax.rsqrt(lax.optimization_barrier(jnp.mean(mix * mix, axis=-1, keepdims=True)) + 1e-05)
    snorm = (mix * rnorm * side_gain).astype(jnp.bfloat16)
    pre = jnp.dot(snorm, w_in, preferred_element_type=jnp.float32)
    hid = jax.nn.silu(pre).astype(jnp.bfloat16)
    side_out = (mix + jnp.dot(hid, w_out, preferred_element_type=jnp.float32)).astype(jnp.bfloat16)
    g_out = lax.dot_general(hid, d_out, (((0,), (0,)), ((), ())), preferred_element_type=jnp.float32)
    dhid = lax.dot_general(d_out, w_out, (((1,), (1,)), ((), ())), preferred_element_type=jnp.float32)
    sig = jax.nn.sigmoid(pre)
    dpre = (dhid * sig * (1.0 + pre * (1.0 - sig))).astype(jnp.bfloat16)
    g_in = lax.dot_general(snorm, dpre, (((0,), (0,)), ((), ())), preferred_element_type=jnp.float32)
    dnorm = lax.dot_general(dpre, w_in, (((1,), (1,)), ((), ())), preferred_element_type=jnp.float32)
    g_gain = lax.optimization_barrier(jnp.sum(dnorm * mix * rnorm, axis=0))
    scaled = dnorm * side_gain
    dmix = d_out.astype(jnp.float32) + rnorm * scaled - mix * rnorm ** 3 * lax.optimization_barrier(jnp.mean(scaled * mix, axis=-1, keepdims=True))
    g_gate = gate * (1.0 - gate) * lax.optimization_barrier(jnp.sum(dmix * (down - prev), axis=0))
    d_prev = (dmix * (1.0 - gate)).astype(jnp.bfloat16)
    d_down = (dmix * gate).astype(jnp.bfloat16)
    g_down = lax.dot_general(ctx, d_down, (((0,), (0,)), ((), ())), preferred_element_type=jnp.float32)
    return (side_out, d_prev, g_down, g_in, g_out, g_gain, g_gate)
```

```python
import jax
import jax.numpy as jnp
import numpy as np
from jax import lax
from jax.experimental import pallas as pl
from jax.experimental.pallas import tpu as pltpu
from jax.sharding import PartitionSpec as P

MESH = pl.DeviceIdType.MESH
F32 = jnp.float32
BF16 = jnp.bfloat16
D = 8192
HD = 128
T = 1024
NT = 32
NDP = 4
SIDE = 1024
EPS = 1e-5
QSCALE = 1.4426950408889634 / np.sqrt(128.0)


def dot(a, b, dims=((1,), (0,))):
    return lax.dot_general(a, b, (dims, ((), ())), preferred_element_type=F32)


def mo(x, n):
    return pl.multiple_of(x, n)


def loop(lo, hi, fn):
    def step(i, carry):
        fn(i)
        return carry

    lax.fori_loop(lo, hi, step, 0)


def sincos(a):
    n = jnp.floor(a * np.float32(2 / np.pi) + 0.5)
    r = a - n * np.float32(1.5703125)
    r = r - n * np.float32(4.837512969970703125e-4)
    r = r - n * np.float32(7.54978995489188216e-8)
    r2 = r * r
    s = r + r * r2 * (-1.6666654611e-1 + r2 * (8.3321608736e-3 - r2 * 1.9515295891e-4))
    c = 1.0 - 0.5 * r2 + r2 * r2 * (
        4.166664568298827e-2 + r2 * (-1.388731625493765e-3 + r2 * 2.443315711809948e-5)
    )
    m = n.astype(jnp.int32)
    odd = (m & 1) == 1
    sin = jnp.where(odd, c, s)
    cos = jnp.where(odd, s, c)
    sin = jnp.where((m & 2) == 2, -sin, sin)
    cos = jnp.where(((m + 1) & 2) == 2, -cos, cos)
    return sin, cos


def kernel(
    x_hbm, wq_hbm, wk_hbm, wv_hbm, wd_hbm,
    gain, seg, freq, win4, woutp, prev, glogit, sgain, dout,
    o_side, o_dprev, o_gdown, o_gin, o_gout, o_gg,
    xbuf, wq, wk, wv, wkv, wd, acc, ssq, scl, cosb, sinb, startb,
    kvown, kvrecv, qbuf, kbuf, vbuf, ctx, ctxt, dsend, drecv,
    win, wout, dout4, snorm4, dns, dnr, sos, sor, ddall, gdf, gds, gdr, gda,
    gsi, gso, r1i, r1o, a2i, a2o, r2i, r2o, o3i, o3o, r3i, r3o, r4i, r4o,
    gv0, gv1, gv2, gv3,
    lsem, xsem,
    kv_s, kv_r, wi_s, wi_r, wo_s, wo_r, wf_s, wf_r, do_s, do_r, rs_s, rs_r,
    sn_s, sn_r, dn_s, dn_r, so_s, so_r, ag_s, ag_r, dr_s, dr_r, da_s, da_r,
    g1_s, g1_r, g2i_s, g2i_r, g2o_s, g2o_r, g3i_s, g3i_r, g3o_s, g3o_r,
    g4i_s, g4i_r, g4o_s, g4o_r, v1_s, v1_r, v2_s, v2_r, v3_s, v3_r,
):
    d = lax.axis_index("dp")
    t = lax.axis_index("tensor")
    core = d % 2
    xh = d // 2
    q = t // 4
    b = t % 4
    yb = t // 8
    sib = xh * 2 + 1 - core

    def rc(src, dst, ss, rs, dd, tt):
        return pltpu.make_async_remote_copy(
            src_ref=src, dst_ref=dst, send_sem=ss, recv_sem=rs,
            device_id=(dd, tt), device_id_type=MESH,
        )

    ld_wk = pltpu.make_async_copy(wk_hbm, wk, lsem.at[0])
    ld_wv = pltpu.make_async_copy(wv_hbm, wv, lsem.at[1])
    ld_wq = pltpu.make_async_copy(wq_hbm, wq, lsem.at[2])
    ld_wd = pltpu.make_async_copy(wd_hbm, wd, lsem.at[3])
    ld_wk.start()
    ld_wv.start()

    def ldx(i):
        rows = pl.ds(mo(i * 256, 256), 256)
        return pltpu.make_async_copy(x_hbm.at[rows], xbuf.at[rows], xsem.at[i])

    loop(0, 4, lambda i: ldx(i).start())
    ld_wq.start()
    ld_wd.start()

    bar = pltpu.get_barrier_semaphore()

    def sig(dd, tt):
        pl.semaphore_signal(bar, inc=1, device_id=(dd, tt), device_id_type=MESH)

    loop(1, NT, lambda j: sig(d, (t + j) % NT))
    sig(sib, t)
    sig((1 - xh) * 2 + 1 - core, t)
    loop(0, 8, lambda j: sig((1 - xh) * 2 + core, 4 * j + b))

    lane = lax.broadcasted_iota(jnp.int32, (1, 128), 1)
    segrow = seg[...].astype(F32)
    segcol = jnp.transpose(jnp.broadcast_to(segrow, (128, T)), (1, 0))

    cnt = jnp.zeros((T, 128), F32)
    for k in range(T // 128):
        cnt = cnt + jnp.where(segrow[:, 128 * k:128 * k + 128] < segcol, 1.0, 0.0)
    start = jnp.sum(cnt, axis=1, keepdims=True)
    tok = lax.broadcasted_iota(jnp.int32, (T, 128), 0).astype(F32)
    startb[...] = jnp.broadcast_to(start, (T, 128))
    sn, cs = sincos((tok - start) * freq[...])
    cosb[...] = cs
    sinb[...] = jnp.where(lane < 64, -sn, sn)

    ri = lax.broadcasted_iota(jnp.int32, (32, 128), 0)
    ci = lax.broadcasted_iota(jnp.int32, (32, 128), 1)
    ek = jnp.where((ci & 63) == ri, 1.0, 0.0).astype(BF16)
    ev = jnp.where((ci & 63) == ri + 32, 1.0, 0.0).astype(BF16)
    ld_wk.wait()
    ld_wv.wait()

    def mkkv(i):
        rows = pl.ds(mo(i * 1024, 1024), 1024)
        wkv[rows, :] = (dot(wk[rows, :], ek) + dot(wv[rows, :], ev)).astype(BF16)

    loop(0, 8, mkkv)

    pl.semaphore_wait(bar, 41)

    hw = pl.ds(mo(core * 256, 256), 256)
    ho = pl.ds(mo(core * 512, 512), 512)

    def c_win(tt):
        return rc(win4.at[tt % 4, :, hw], win.at[pl.ds(mo(32 * t, 32), 32), hw], wi_s.at[tt], wi_r.at[t], d, tt)

    def c_win_in(ss):
        return rc(win4.at[0, :, hw], win.at[pl.ds(mo(32 * ss, 32), 32), hw], wi_s.at[ss], wi_r.at[ss], d, ss)

    loop(1, NT, lambda j: c_win((t + j) % NT).start())
    win[pl.ds(mo(32 * t, 32), 32), hw] = win4[b, :, hw]
    wb = t // 8
    wj = t % 8

    def c_wout(qq):
        return rc(woutp.at[:, ho], wout.at[pl.ds(mo(64 * wj, 64), 64), ho], wo_s.at[qq], wo_r.at[wj], d, 4 * qq + wb)

    def c_wout_in(jj):
        return rc(woutp.at[:, ho], wout.at[pl.ds(mo(64 * jj, 64), 64), ho], wo_s.at[jj], wo_r.at[jj], d, 8 * b + jj)

    def start_wout(qq):
        @pl.when(4 * qq + wb != t)
        def _():
            c_wout(qq).start()

    loop(0, 8, start_wout)

    @pl.when(wb == b)
    def _():
        @pl.when(q * 4 + wb == t)
        def _():
            wout[pl.ds(mo(64 * wj, 64), 64), ho] = woutp[:, ho]

    def qd(src, dst, ss, rs, j):
        bb = (b + j) % 4
        return rc(src, dst, ss.at[bb], rs.at[b], d, 4 * q + bb)

    def qd_in(src, dst, ss, rs, j):
        bb = (b + j) % 4
        return rc(src, dst, ss.at[bb], rs.at[bb], d, 4 * q + bb)

    own32 = pl.ds(mo(32 * b, 32), 32)
    loop(1, 4, lambda j: qd(dout, dout4.at[own32], do_s, do_r, j).start())
    dout4[own32, :] = dout[...]

    def kv_chunk(i):
        rows = pl.ds(mo(i * 256, 256), 256)
        ldx(i).wait()
        acc[...] = jnp.zeros((256, 128), F32)
        ssq[...] = jnp.zeros((256, 128), F32)

        def kk(k):
            cols = pl.ds(mo(k * 1024, 1024), 1024)
            xb = xbuf[rows, cols].astype(F32)
            sq = xb * xb
            part = sq[:, 0:128]
            for m in range(1, 8):
                part = part + sq[:, 128 * m:128 * m + 128]
            ssq[...] = ssq[...] + part
            xg = (xb * gain[:, cols]).astype(BF16)
            xbuf[rows, cols] = xg
            acc[...] = acc[...] + dot(xg, wkv[cols, :])

        loop(0, 8, kk)
        s = lax.rsqrt(jnp.sum(ssq[...], axis=1, keepdims=True) * (1.0 / D) + EPS)
        sb = jnp.broadcast_to(s, (256, 128))
        scl[rows, :] = sb
        kv = acc[...] * sb
        piece = jnp.where(lane < 64, kv[0:128], kv[128:256]).astype(BF16)
        prow = pl.ds(mo(i * 128, 128), 128)
        kvown[prow, :] = piece
        kvrecv[b, prow, :] = piece
        loop(1, 4, lambda j: rc(
            kvown.at[prow], kvrecv.at[b, prow], kv_s.at[i, (b + j) % 4], kv_r.at[i, b], d, 4 * q + (b + j) % 4
        ).start())

    loop(0, 4, kv_chunk)

    ld_wq.wait()

    def q_chunk(i):
        rows = pl.ds(mo(i * 256, 256), 256)
        qv = dot(xbuf[rows, :], wq[...])
        sb = scl[rows, :] * np.float32(QSCALE)
        co = cosb[rows, :] * sb
        si = sinb[rows, :] * sb
        for h in range(2):
            v = qv[:, 128 * h:128 * h + 128]
            qbuf[h, rows, :] = (v * co + pltpu.roll(v, 64, 1) * si).astype(BF16)

    loop(0, 4, q_chunk)

    def kv_in(i, j):
        bb = (b + j) % 4
        prow = pl.ds(mo(i * 128, 128), 128)
        rc(kvown.at[prow], kvrecv.at[bb, prow], kv_s.at[i, bb], kv_r.at[i, bb], d, 4 * q + bb).wait_recv()

    loop(0, 4, lambda i: loop(1, 4, lambda j: kv_in(i, j)))
    er = lax.broadcasted_iota(jnp.int32, (128, 512), 0)
    ec = lax.broadcasted_iota(jnp.int32, (128, 512), 1)
    base = ((er >> 6) << 8) + (((er >> 5) & 1) << 7) + (er & 31)

    def kv_build(i):
        prow = pl.ds(mo(i * 128, 128), 128)
        m = jnp.zeros((128, 512), F32)
        for bb in range(4):
            sel = jnp.where(ec == base + 32 * bb, 1.0, 0.0).astype(BF16)
            m = m + dot(kvrecv[bb, prow, :], sel)
        for h in range(2):
            rows = pl.ds(mo(i * 256 + h * 128, 128), 128)
            kf = m[:, 256 * h:256 * h + 128]
            kbuf[rows, :] = (kf * cosb[rows, :] + pltpu.roll(kf, 64, 1) * sinb[rows, :]).astype(BF16)
            vbuf[rows, 0:128] = m[:, 256 * h + 128:256 * h + 256].astype(BF16)
            vbuf[rows, 128:256] = jnp.ones((128, 128), BF16)

    loop(0, 4, kv_build)
    ld_wd.wait()

    def rs_dst(i, m):
        return i * 8 + (m + wj) % 8

    def rs_copy(tt):
        return rc(dsend.at[tt], drecv.at[t], rs_s.at[tt], rs_r.at[t], d, tt)

    def attn(j):
        i = (yb + 1 + j) % 4
        rows = pl.ds(mo(i * 256, 256), 256)
        k0 = mo(jnp.maximum(i - 2, 0) * 256, 256)
        keys = pl.ds(k0, 768)
        kw = kbuf[keys, :]
        vw = vbuf[keys, :]
        kidx = lax.broadcasted_iota(jnp.int32, (256, 768), 1) + k0
        qidx = lax.broadcasted_iota(jnp.int32, (256, 768), 0) + i * 256
        lo = startb[rows, 0:1].astype(jnp.int32)
        ok = (kidx <= qidx) & (kidx >= lo)
        for h in range(2):
            sc = dot(qbuf[h, rows, :], kw, ((1,), (1,)))
            p = jnp.where(ok, jnp.exp2(sc), 0.0).astype(BF16)
            o = dot(p, vw)
            ctx[rows, 128 * h:128 * h + 128] = (o[:, 0:128] / o[:, 128:256]).astype(BF16)
        down = dot(ctx[rows, :], wd[...]).astype(BF16)
        for m in range(8):
            dsend[i * 8 + m] = down[32 * m:32 * m + 32, :]

        def go(m):
            tt = rs_dst(i, m)

            @pl.when(tt != t)
            def _():
                rs_copy(tt).start()

        loop(0, 8, go)

    loop(0, 4, attn)
    drecv[t] = dsend[t]

    loop(1, NT, lambda j: c_win_in((t + j) % NT).wait_recv())

    def wait_wout(jj):
        @pl.when(8 * b + jj != t)
        def _():
            c_wout_in(jj).wait_recv()

    loop(0, 8, wait_wout)
    fw1 = rc(win.at[:, hw], win.at[:, hw], wf_s.at[0], wf_r.at[0], sib, t)
    fw2 = rc(wout.at[:, ho], wout.at[:, ho], wf_s.at[1], wf_r.at[1], sib, t)
    fw1.start()
    fw2.start()

    def ctx_t(i):
        rows = pl.ds(mo(i * 256, 256), 256)
        ctxt[:, rows] = jnp.transpose(ctx[rows, :].astype(F32), (1, 0)).astype(BF16)

    loop(0, 4, ctx_t)
    loop(1, 4, lambda j: qd_in(dout, dout4.at[pl.ds(mo(32 * ((b + j) % 4), 32), 32)], do_s, do_r, j).wait_recv())
    fw1.wait_recv()
    fw2.wait_recv()
    dhid = dot(dout4[...], wout[...], ((1,), (1,)))

    loop(1, NT, lambda j: rc(
        dsend.at[(t + j) % NT], drecv.at[(t + j) % NT], rs_s.at[(t + j) % NT], rs_r.at[(t + j) % NT], d, (t + j) % NT
    ).wait_recv())
    down = lax.fori_loop(0, NT, lambda s, a: a + drecv[s].astype(F32), jnp.zeros((32, SIDE), F32))
    gate = jax.nn.sigmoid(glogit[...])
    prv = prev[...].astype(F32)
    mix = gate * down + (1.0 - gate) * prv
    r = lax.rsqrt(jnp.mean(mix * mix, axis=1, keepdims=True) + EPS)
    snorm4[own32, :] = (mix * r * sgain[...]).astype(BF16)
    loop(1, 4, lambda j: qd(snorm4.at[own32], snorm4.at[own32], sn_s, sn_r, j).start())

    def in32(j):
        return pl.ds(mo(32 * ((b + j) % 4), 32), 32)

    loop(1, 4, lambda j: qd_in(snorm4.at[in32(j)], snorm4.at[in32(j)], sn_s, sn_r, j).wait_recv())

    sn4 = snorm4[...]
    pre = dot(sn4, win[...])
    sig_pre = jax.nn.sigmoid(pre)
    hid = (pre * sig_pre).astype(BF16)
    dpre = (dhid * sig_pre * (1.0 + pre * (1.0 - sig_pre))).astype(BF16)
    dnp = dot(dpre, win[...], ((1,), (1,))).astype(BF16)
    for bb in range(4):
        dns[bb] = dnp[32 * bb:32 * bb + 32, :]
    loop(1, 4, lambda j: qd(dns.at[(b + j) % 4], dnr.at[b], dn_s, dn_r, j).start())
    dnr[b] = dns[b]
    sop = dot(hid, wout[...]).astype(BF16)
    for bb in range(4):
        sos[bb] = sop[32 * bb:32 * bb + 32, :]
    loop(1, 4, lambda j: qd(sos.at[(b + j) % 4], sor.at[b], so_s, so_r, j).start())
    sor[b] = sos[b]
    gin_l = dot(sn4, dpre, ((0,), (0,))).astype(BF16)
    for dd in range(4):
        gsi[dd] = gin_l[:, 128 * dd:128 * dd + 128]
    gout_l = dot(hid, dout4[...], ((0,), (0,))).astype(BF16)
    for dd in range(4):
        gso[dd] = gout_l[:, 256 * dd:256 * dd + 256]

    loop(1, 4, lambda j: qd_in(dns.at[0], dnr.at[(b + j) % 4], dn_s, dn_r, j).wait_recv())
    dn = (dnr[0].astype(F32) + dnr[1].astype(F32)) + (dnr[2].astype(F32) + dnr[3].astype(F32))
    scaled = dn * sgain[...]
    dmix = (
        dout[...].astype(F32)
        + r * scaled
        - mix * (r * r * r) * jnp.mean(scaled * mix, axis=1, keepdims=True)
    )
    dd_rows = pl.ds(mo(32 * t, 32), 32)
    ddall[dd_rows, :] = (dmix * gate).astype(BF16)
    loop(1, NT, lambda j: rc(
        ddall.at[dd_rows], ddall.at[dd_rows], ag_s.at[(t + j) % NT], ag_r.at[t], d, (t + j) % NT
    ).start())
    o_dprev[...] = (dmix * (1.0 - gate)).astype(BF16)
    gv0[b, :, 0:SIDE] = jnp.sum(dn * mix * r, axis=0, keepdims=True)
    gv0[b, :, SIDE:] = gate * (1.0 - gate) * jnp.sum(dmix * (down - prv), axis=0, keepdims=True)
    loop(1, 4, lambda j: qd(gv0.at[b], gv0.at[b], v1_s, v1_r, j).start())

    def g1(xx, k):
        if k == 0:
            return rc(gsi.at[2 * xx + 1 - core], r1i.at[xx], g1_s.at[0, xx], g1_r.at[0, xx], sib, t)
        return rc(gso.at[2 * xx + 1 - core], r1o.at[xx], g1_s.at[1, xx], g1_r.at[1, xx], sib, t)

    for k in range(2):
        for xx in range(2):
            g1(xx, k).start()

    loop(1, 4, lambda j: qd_in(sos.at[0], sor.at[(b + j) % 4], so_s, so_r, j).wait_recv())
    o_side[...] = (
        mix + ((sor[0].astype(F32) + sor[1].astype(F32)) + (sor[2].astype(F32) + sor[3].astype(F32)))
    ).astype(BF16)

    loop(1, 4, lambda j: qd_in(gv0.at[0], gv0.at[(b + j) % 4], v1_s, v1_r, j).wait_recv())
    gv1[...] = (gv0[0] + gv0[1]) + (gv0[2] + gv0[3])
    cv2 = rc(gv1, gv2, v2_s, v2_r, sib, t)
    cv2.start()

    for xx in range(2):
        g1(xx, 0).wait_recv()
        a2i[xx] = (gsi[2 * xx + core].astype(F32) + r1i[xx].astype(F32)).astype(BF16)
    for xx in range(2):
        g1(xx, 1).wait_recv()
        a2o[xx] = (gso[2 * xx + core].astype(F32) + r1o[xx].astype(F32)).astype(BF16)
    cv2.wait_recv()
    me16 = xh * 8 + q
    gv3[me16] = gv1[...] + gv2[...]

    def peer(j):
        return (me16 + j) % 16

    def g2(p, src, k):
        xx = p // 8
        qq = p % 8
        dev = (2 * xx + core, 4 * qq + b)
        if k == 0:
            return rc(a2i.at[xx, pl.ds(mo(128 * qq, 128), 128)], r2i.at[src], g2i_s.at[p], g2i_r.at[src], *dev)
        if k == 1:
            return rc(a2o.at[xx, pl.ds(mo(64 * qq, 64), 64)], r2o.at[src], g2o_s.at[p], g2o_r.at[src], *dev)
        return rc(gv3.at[me16], gv3.at[src], v3_s.at[p], v3_r.at[src], *dev)

    for k in range(3):
        loop(1, 16, lambda j, k=k: g2(peer(j), me16, k).start())
    r2i[me16] = a2i[xh, pl.ds(mo(128 * q, 128), 128), :]
    r2o[me16] = a2o[xh, pl.ds(mo(64 * q, 64), 64), :]

    loop(1, NT, lambda j: rc(
        ddall.at[dd_rows], ddall.at[pl.ds(mo(32 * ((t + j) % NT), 32), 32)], ag_s.at[(t + j) % NT], ag_r.at[(t + j) % NT], d, (t + j) % NT
    ).wait_recv())
    gdf[...] = dot(ctxt[...], ddall[...]).astype(BF16)

    def dpc(src, dst, ss, rs, slot, j):
        dd = (d + j) % 4
        return rc(src, dst, ss.at[dd], rs.at[slot], dd, t)

    def q64(dd):
        return pl.ds(mo(64 * dd, 64), 64)

    loop(1, 4, lambda j: dpc(gdf.at[q64((d + j) % 4)], gdr.at[d], dr_s, dr_r, d, j).start())
    gdr[d] = gdf[q64(d), :]

    for k in range(3):
        loop(1, 16, lambda j, k=k: g2(peer(j), peer(j), k).wait_recv())
    oi = lax.fori_loop(0, 16, lambda s, a: a + r2i[s].astype(F32), jnp.zeros((128, 128), F32))
    oo = lax.fori_loop(0, 16, lambda s, a: a + r2o[s].astype(F32), jnp.zeros((64, 256), F32))
    o3i[...] = oi.astype(BF16)
    o3o[...] = oo.astype(BF16)
    r3i[b] = o3i[own32, :]
    loop(1, 4, lambda j: qd(o3i.at[in32(j)], r3i.at[b], g3i_s, g3i_r, j).start())
    to_t = 8 * b + q
    from_t = 4 * wj + wb
    co3 = rc(o3o, r3o, g3o_s, g3o_r, d, to_t)

    @pl.when(to_t != t)
    def _():
        co3.start()

    @pl.when(to_t == t)
    def _():
        r3o[...] = o3o[...]

    o_gg[...] = lax.fori_loop(0, 16, lambda s, a: a + gv3[s], jnp.zeros((1, 2 * SIDE), F32))

    loop(1, 4, lambda j: dpc(gdf.at[q64(d)], gdr.at[(d + j) % 4], dr_s, dr_r, (d + j) % 4, j).wait_recv())
    gda[q64(d), :] = (
        (gdr[0].astype(F32) + gdr[1].astype(F32)) + (gdr[2].astype(F32) + gdr[3].astype(F32))
    ).astype(BF16)
    loop(1, 4, lambda j: dpc(gda.at[q64(d)], gda.at[q64(d)], da_s, da_r, d, j).start())

    loop(1, 4, lambda j: qd_in(o3i.at[own32], r3i.at[(b + j) % 4], g3i_s, g3i_r, j).wait_recv())

    @pl.when(from_t != t)
    def _():
        rc(o3o, r3o, g3o_s, g3o_r, d, from_t).wait_recv()

    r4i[d] = r3i[...]
    r4o[d] = r3o[...]
    loop(1, 4, lambda j: dpc(r4i.at[d], r4i.at[d], g4i_s, g4i_r, d, j).start())
    loop(1, 4, lambda j: dpc(r4o.at[d], r4o.at[d], g4o_s, g4o_r, d, j).start())

    loop(1, 4, lambda j: dpc(gda.at[q64(d)], gda.at[q64((d + j) % 4)], da_s, da_r, (d + j) % 4, j).wait_recv())
    o_gdown[...] = gda[...].astype(F32)
    loop(1, 4, lambda j: dpc(r4i.at[d], r4i.at[(d + j) % 4], g4i_s, g4i_r, (d + j) % 4, j).wait_recv())
    loop(1, 4, lambda j: dpc(r4o.at[d], r4o.at[(d + j) % 4], g4o_s, g4o_r, (d + j) % 4, j).wait_recv())
    for dd in range(4):
        for bb in range(4):
            o_gin[:, 512 * bb + 128 * dd:512 * bb + 128 * dd + 128] = r4i[dd, bb].astype(F32)
        o_gout[:, 256 * dd:256 * dd + 256] = r4o[dd].astype(F32)

    loop(1, NT, lambda j: c_win((t + j) % NT).wait_send())

    def wout_sent(qq):
        @pl.when(4 * qq + wb != t)
        def _():
            c_wout(qq).wait_send()

    loop(0, 8, wout_sent)
    fw1.wait_send()
    fw2.wait_send()
    loop(1, 4, lambda j: qd(dout, dout4.at[own32], do_s, do_r, j).wait_send())

    def kv_sent(i):
        prow = pl.ds(mo(i * 128, 128), 128)
        loop(1, 4, lambda j: rc(
            kvown.at[prow], kvrecv.at[b, prow], kv_s.at[i, (b + j) % 4], kv_r.at[i, b], d, 4 * q + (b + j) % 4
        ).wait_send())

    loop(0, 4, kv_sent)
    loop(1, NT, lambda j: rs_copy((t + j) % NT).wait_send())
    loop(1, 4, lambda j: qd(snorm4.at[own32], snorm4.at[own32], sn_s, sn_r, j).wait_send())
    loop(1, 4, lambda j: qd(dns.at[(b + j) % 4], dnr.at[b], dn_s, dn_r, j).wait_send())
    loop(1, 4, lambda j: qd(sos.at[(b + j) % 4], sor.at[b], so_s, so_r, j).wait_send())
    loop(1, NT, lambda j: rc(
        ddall.at[dd_rows], ddall.at[dd_rows], ag_s.at[(t + j) % NT], ag_r.at[t], d, (t + j) % NT
    ).wait_send())
    loop(1, 4, lambda j: qd(gv0.at[b], gv0.at[b], v1_s, v1_r, j).wait_send())
    for k in range(2):
        for xx in range(2):
            g1(xx, k).wait_send()
    cv2.wait_send()
    for k in range(3):
        loop(1, 16, lambda j, k=k: g2(peer(j), me16, k).wait_send())
    loop(1, 4, lambda j: dpc(gdf.at[q64((d + j) % 4)], gdr.at[d], dr_s, dr_r, d, j).wait_send())
    loop(1, 4, lambda j: qd(o3i.at[in32(j)], r3i.at[b], g3i_s, g3i_r, j).wait_send())

    @pl.when(to_t != t)
    def _():
        co3.wait_send()

    loop(1, 4, lambda j: dpc(gda.at[q64(d)], gda.at[q64(d)], da_s, da_r, d, j).wait_send())
    loop(1, 4, lambda j: dpc(r4i.at[d], r4i.at[d], g4i_s, g4i_r, d, j).wait_send())
    loop(1, 4, lambda j: dpc(r4o.at[d], r4o.at[d], g4o_s, g4o_r, d, j).wait_send())


def body(
    hidden_in, attn_gain, seg_ids, w_query, w_key, w_value, w_down,
    prev_side, gate_logit, side_gain, w_in, w_out, d_out,
):
    half = HD // 2
    fr = (10000.0 ** (-np.arange(half) * 2.0 / HD)).astype(np.float32)
    freq = jnp.asarray(np.concatenate([fr, fr])[None])
    win4 = jnp.pad(w_in.reshape(32, 4, 8, 56), ((0, 0), (0, 0), (0, 0), (0, 8)))
    win4 = win4.reshape(32, 4, 512).transpose(1, 0, 2)
    woutp = jnp.pad(w_out, ((0, 8), (0, 0)))
    vm = pl.BlockSpec(memory_space=pltpu.VMEM)
    anym = pl.BlockSpec(memory_space=pl.ANY)
    dma = pltpu.SemaphoreType.DMA

    def V(shape, dt=BF16):
        return pltpu.VMEM(shape, dt)

    scratch = [
        V((T, D)), V((D, 256)), V((D, 32)), V((D, 32)), V((D, 128)), V((256, SIDE)),
        V((256, 128), F32), V((256, 128), F32), V((T, 128), F32), V((T, 128), F32), V((T, 128), F32), V((T, 128), F32),
        V((512, 128)), V((4, 512, 128)), V((2, T, 128)), V((T, 128)), V((T, 256)), V((T, 256)), V((256, T)),
        V((NT, 32, SIDE)), V((NT, 32, SIDE)),
        V((SIDE, 512)), V((512, SIDE)), V((128, SIDE)), V((128, SIDE)),
        V((4, 32, SIDE)), V((4, 32, SIDE)), V((4, 32, SIDE)), V((4, 32, SIDE)),
        V((T, SIDE)), V((256, SIDE)), V((8, 128)), V((4, 64, SIDE)), V((256, SIDE)),
        V((4, SIDE, 128)), V((4, 512, 256)), V((2, SIDE, 128)), V((2, 512, 256)), V((2, SIDE, 128)), V((2, 512, 256)),
        V((16, 128, 128)), V((16, 64, 256)), V((128, 128)), V((64, 256)), V((4, 32, 128)), V((64, 256)),
        V((4, 4, 32, 128)), V((4, 64, 256)),
        V((4, 1, 2 * SIDE), F32), V((1, 2 * SIDE), F32), V((1, 2 * SIDE), F32), V((16, 1, 2 * SIDE), F32),
        dma((4,)), dma((4,)),
        dma((4, 4)), dma((4, 4)), dma((32,)), dma((32,)), dma((8,)), dma((8,)), dma((2,)), dma((2,)),
        dma((4,)), dma((4,)), dma((32,)), dma((32,)),
        dma((4,)), dma((4,)), dma((4,)), dma((4,)), dma((4,)), dma((4,)), dma((32,)), dma((32,)),
        dma((4,)), dma((4,)), dma((4,)), dma((4,)),
        dma((2, 2)), dma((2, 2)), dma((16,)), dma((16,)), dma((16,)), dma((16,)), dma((4,)), dma((4,)), dma, dma,
        dma((4,)), dma((4,)), dma((4,)), dma((4,)), dma((4,)), dma((4,)), dma, dma, dma((16,)), dma((16,)),
    ]
    out = pl.pallas_call(
        kernel,
        out_shape=(
            jax.ShapeDtypeStruct((32, SIDE), BF16),
            jax.ShapeDtypeStruct((32, SIDE), BF16),
            jax.ShapeDtypeStruct((256, SIDE), F32),
            jax.ShapeDtypeStruct((32, 2048), F32),
            jax.ShapeDtypeStruct((64, SIDE), F32),
            jax.ShapeDtypeStruct((1, 2 * SIDE), F32),
        ),
        in_specs=[anym] * 5 + [vm] * 9,
        out_specs=tuple([vm] * 6),
        scratch_shapes=scratch,
        compiler_params=pltpu.CompilerParams(
            collective_id=0, has_side_effects=True, vmem_limit_bytes=60 * 1024 * 1024
        ),
    )(
        hidden_in, w_query, w_key, w_value, w_down,
        attn_gain[None], seg_ids[None], freq, win4, woutp, prev_side, gate_logit[None], side_gain[None], d_out,
    )
    side_out, d_prev, g_down, gin, gout, gg = out
    g_in = gin.reshape(32, 32, 64)[:, :, :56].reshape(32, 1792)
    g_out = gout[:56]
    rank = lax.axis_index("tensor")
    g_gain = lax.dynamic_slice_in_dim(gg[0, :SIDE], rank * 32, 32, 0)
    g_gate = lax.dynamic_slice_in_dim(gg[0, SIDE:], rank * 32, 32, 0)
    return side_out, d_prev, g_down, g_in, g_out, g_gain, g_gate


def solution(mesh):
    return jax.shard_map(
        body,
        mesh=mesh,
        in_specs=(
            P("dp", None), P(), P("dp"), P(None, "tensor"), P(None, "tensor"), P(None, "tensor"),
            P("tensor", None), P(("dp", "tensor"), None), P(), P(), P("tensor", None), P("tensor", None),
            P(("dp", "tensor"), None),
        ),
        out_specs=(
            P(("dp", "tensor"), None), P(("dp", "tensor"), None), P("tensor", None), P("tensor", None),
            P("tensor", None), P("tensor"), P("tensor"),
        ),
        check_vma=False,
    )
```

```python
import jax
import jax.numpy as jnp
import numpy as np
from jax import lax
from jax.experimental import pallas as pl
from jax.experimental.pallas import tpu as pltpu
from jax.sharding import PartitionSpec as P

MESH = pl.DeviceIdType.MESH
F32 = jnp.float32
BF16 = jnp.bfloat16
D = 8192
HD = 128
T = 1024
NT = 32
NDP = 4
SIDE = 1024
EPS = 1e-5
QSCALE = 1.4426950408889634 / np.sqrt(128.0)


def dot(a, b, dims=((1,), (0,))):
    return lax.dot_general(a, b, (dims, ((), ())), preferred_element_type=F32)


def mo(x, n):
    return pl.multiple_of(x, n)


def loop(lo, hi, fn):
    def step(i, carry):
        fn(i)
        return carry

    lax.fori_loop(lo, hi, step, 0)


def sincos(a):
    n = jnp.floor(a * np.float32(2 / np.pi) + 0.5)
    r = a - n * np.float32(1.5703125)
    r = r - n * np.float32(4.837512969970703125e-4)
    r = r - n * np.float32(7.54978995489188216e-8)
    r2 = r * r
    s = r + r * r2 * (-1.6666654611e-1 + r2 * (8.3321608736e-3 - r2 * 1.9515295891e-4))
    c = 1.0 - 0.5 * r2 + r2 * r2 * (
        4.166664568298827e-2 + r2 * (-1.388731625493765e-3 + r2 * 2.443315711809948e-5)
    )
    m = n.astype(jnp.int32)
    odd = (m & 1) == 1
    sin = jnp.where(odd, c, s)
    cos = jnp.where(odd, s, c)
    sin = jnp.where((m & 2) == 2, -sin, sin)
    cos = jnp.where(((m + 1) & 2) == 2, -cos, cos)
    return sin, cos


def kernel(
    x_hbm, wq_hbm, wk_hbm, wv_hbm, wd_hbm,
    gain, seg, freq, win4, woutp, prev, glogit, sgain, dout,
    o_side, o_dprev, o_gdown, o_gin, o_gout, o_gg,
    xbuf, wq, wk, wv, wkv, wd4, acc, accq, ssq, cosb, sinb, startb,
    kvown, kvrecv, qbuf, kbuf, vbuf, csend, ctx4, ctxt, dsend, drecv,
    win, wout, dout4, snorm4, dns, dnr, sos, sor, ddall, gds, h1r, h2s, h2r, gda,
    gsi, gso, r1i, r1o, a2i, a2o, r2i, r2o, o3i, o3o, r3i, r3o, r4i, r4o,
    gv0, gv1, gv2, gv3,
    lsem, xsem,
    kv_s, kv_r, wi_s, wi_r, wo_s, wo_r, wf_s, wf_r, do_s, do_r, rs_s, rs_r, wd_s, wd_r, wg_s, wg_r, ca_s, ca_r,
    sn_s, sn_r, dn_s, dn_r, so_s, so_r, ag_s, ag_r, h1_s, h1_r, h2_s, h2_r, da_s, da_r,
    g1_s, g1_r, g2i_s, g2i_r, g2o_s, g2o_r, g3i_s, g3i_r, g3o_s, g3o_r,
    g4i_s, g4i_r, g4o_s, g4o_r, v1_s, v1_r, v2_s, v2_r, v3_s, v3_r,
):
    d = lax.axis_index("dp")
    t = lax.axis_index("tensor")
    core = d % 2
    xh = d // 2
    q = t // 4
    b = t % 4
    yb = t // 8
    sib = xh * 2 + 1 - core

    def rc(src, dst, ss, rs, dd, tt):
        return pltpu.make_async_remote_copy(
            src_ref=src, dst_ref=dst, send_sem=ss, recv_sem=rs,
            device_id=(dd, tt), device_id_type=MESH,
        )

    ld_wk = pltpu.make_async_copy(wk_hbm, wk, lsem.at[0])
    ld_wv = pltpu.make_async_copy(wv_hbm, wv, lsem.at[1])
    ld_wq = pltpu.make_async_copy(wq_hbm, wq, lsem.at[2])
    ld_wd = pltpu.make_async_copy(wd_hbm, wd4.at[yb], lsem.at[3])
    ld_wd.start()
    ld_wk.start()
    ld_wv.start()

    def ldx(i):
        rows = pl.ds(mo(i * 256, 256), 256)
        return pltpu.make_async_copy(x_hbm.at[rows], xbuf.at[rows], xsem.at[i])

    ld_wq.start()
    ldx(0).start()

    bar = pltpu.get_barrier_semaphore()

    def sig(dd, tt):
        pl.semaphore_signal(bar, inc=1, device_id=(dd, tt), device_id_type=MESH)

    loop(1, NT, lambda j: sig(d, (t + j) % NT))
    sig(sib, t)
    sig((1 - xh) * 2 + 1 - core, t)
    loop(0, 8, lambda j: sig((1 - xh) * 2 + core, 4 * j + b))

    ld_wd.wait()
    pl.semaphore_wait(bar, 41)

    t8 = t % 8
    hr = pl.ds(mo(128 * core, 128), 128)

    def yr(src, dst, ss, rs, j):
        yy = (yb + j) % 4
        return rc(src, dst, ss.at[yy], rs.at[yb], d, 8 * yy + t8)

    def yr_in(src, dst, ss, rs, j):
        yy = (yb + j) % 4
        return rc(src, dst, ss.at[yy], rs.at[yy], d, 8 * yy + t8)

    def c_wd(j):
        return yr(wd4.at[yb, hr], wd4.at[yb, hr], wd_s, wd_r, j)

    loop(1, 4, lambda j: c_wd(j).start())

    def c_win(tt):
        return rc(win4.at[tt % 4, core], win.at[core, pl.ds(mo(32 * t, 32), 32)], wi_s.at[tt], wi_r.at[t], d, tt)

    def c_win_in(ss):
        return rc(win4.at[0, core], win.at[core, pl.ds(mo(32 * ss, 32), 32)], wi_s.at[ss], wi_r.at[ss], d, ss)

    wb = t // 8
    wj = t % 8

    def c_wout(qq):
        return rc(woutp.at[core], wout.at[core, pl.ds(mo(64 * wj, 64), 64)], wo_s.at[qq], wo_r.at[wj], d, 4 * qq + wb)

    def c_wout_in(jj):
        return rc(woutp.at[core], wout.at[core, pl.ds(mo(64 * jj, 64), 64)], wo_s.at[jj], wo_r.at[jj], d, 8 * b + jj)

    def start_wout(j):
        qq = (q + j) % 8

        @pl.when(4 * qq + wb != t)
        def _():
            c_wout(qq).start()

    loop(0, 8, start_wout)

    @pl.when(wb == b)
    def _():
        wout[core, pl.ds(mo(64 * wj, 64), 64), :] = woutp[core]

    def qd(src, dst, ss, rs, j):
        bb = (b + j) % 4
        return rc(src, dst, ss.at[bb], rs.at[b], d, 4 * q + bb)

    def qd_in(src, dst, ss, rs, j):
        bb = (b + j) % 4
        return rc(src, dst, ss.at[bb], rs.at[bb], d, 4 * q + bb)

    own32 = pl.ds(mo(32 * b, 32), 32)
    loop(1, 4, lambda j: qd(dout, dout4.at[own32], do_s, do_r, j).start())
    dout4[own32, :] = dout[...]

    lane = lax.broadcasted_iota(jnp.int32, (1, 128), 1)
    segrow = seg[...].astype(F32)
    segcol = jnp.transpose(jnp.broadcast_to(segrow, (128, T)), (1, 0))
    cnt = jnp.zeros((T, 128), F32)
    for k in range(T // 128):
        cnt = cnt + jnp.where(segrow[:, 128 * k:128 * k + 128] < segcol, 1.0, 0.0)
    start = jnp.sum(cnt, axis=1, keepdims=True)
    tok = lax.broadcasted_iota(jnp.int32, (T, 128), 0).astype(F32)
    startb[...] = jnp.broadcast_to(start, (T, 128))
    sn, cs = sincos((tok - start) * freq[...])
    cosb[...] = cs
    sinb[...] = jnp.where(lane < 64, -sn, sn)

    ld_wk.wait()
    ld_wv.wait()
    gk = (wk[...].astype(F32) * gain[...]).astype(BF16)
    gvw = (wv[...].astype(F32) * gain[...]).astype(BF16)
    wkv[0:32, :] = gk
    wkv[32:64, :] = gvw
    wkv[64:96, :] = gk
    wkv[96:128, :] = gvw
    ld_wq.wait()

    def gain_q(i):
        rows = pl.ds(mo(i * 1024, 1024), 1024)
        gcol = jnp.transpose(jnp.broadcast_to(gain[:, rows], (128, 1024)), (1, 0))
        for h in range(2):
            hh = slice(128 * h, 128 * h + 128)
            wq[rows, hh] = (wq[rows, hh].astype(F32) * gcol).astype(BF16)

    ldx(1).start()
    loop(0, 8, gain_q)

    def kv_chunk(i):
        rows = pl.ds(mo(i * 256, 256), 256)
        ldx(i).wait()

        @pl.when(i < 2)
        def _():
            ldx(i + 2).start()

        acc[...] = jnp.zeros((256, 128), F32)
        accq[...] = jnp.zeros((256, 256), F32)
        ssq[...] = jnp.zeros((256, 128), F32)

        def kk(k):
            cols = pl.ds(mo(k * 2048, 2048), 2048)
            xb = xbuf[rows, cols]
            xf = xb.astype(F32)
            sq = xf * xf
            part = sq[:, 0:128]
            for m in range(1, 16):
                part = part + sq[:, 128 * m:128 * m + 128]
            ssq[...] = ssq[...] + part
            acc[...] = acc[...] + dot(xb, wkv[:, cols], ((1,), (1,)))
            accq[...] = accq[...] + dot(xb, wq[cols, :])

        loop(0, 4, kk)
        s = lax.rsqrt(jnp.sum(ssq[...], axis=1, keepdims=True) * (1.0 / D) + EPS)
        sb = jnp.broadcast_to(s, (256, 128))
        kv = acc[...] * sb
        piece = jnp.where(lane < 64, kv[0:128], kv[128:256]).astype(BF16)
        prow = pl.ds(mo(i * 128, 128), 128)
        kvown[prow, :] = piece
        kvrecv[b, prow, :] = piece
        loop(1, 4, lambda j: rc(
            kvown.at[prow], kvrecv.at[b, prow], kv_s.at[i, (b + j) % 4], kv_r.at[i, b], d, 4 * q + (b + j) % 4
        ).start())
        sb = sb * np.float32(QSCALE)
        co = cosb[rows, :] * sb
        si = sinb[rows, :] * sb
        for h in range(2):
            v = accq[:, 128 * h:128 * h + 128]
            qbuf[h, rows, :] = (v * co + pltpu.roll(v, 64, 1) * si).astype(BF16)

    loop(0, 4, kv_chunk)
    loop(1, NT, lambda j: c_win((t + j) % NT).start())
    win[core, pl.ds(mo(32 * t, 32), 32), :] = win4[b, core]

    def kv_in(i, j):
        bb = (b + j) % 4
        prow = pl.ds(mo(i * 128, 128), 128)
        rc(kvown.at[prow], kvrecv.at[bb, prow], kv_s.at[i, bb], kv_r.at[i, bb], d, 4 * q + bb).wait_recv()

    loop(0, 4, lambda i: loop(1, 4, lambda j: kv_in(i, j)))
    er = lax.broadcasted_iota(jnp.int32, (128, 512), 0)
    ec = lax.broadcasted_iota(jnp.int32, (128, 512), 1)
    base = ((er >> 6) << 8) + (((er >> 5) & 1) << 7) + (er & 31)

    def kv_build(i):
        prow = pl.ds(mo(i * 128, 128), 128)
        m = jnp.zeros((128, 512), F32)
        for bb in range(4):
            sel = jnp.where(ec == base + 32 * bb, 1.0, 0.0).astype(BF16)
            m = m + dot(kvrecv[bb, prow, :], sel)
        for h in range(2):
            rows = pl.ds(mo(i * 256 + h * 128, 128), 128)
            kf = m[:, 256 * h:256 * h + 128]
            kbuf[rows, :] = (kf * cosb[rows, :] + pltpu.roll(kf, 64, 1) * sinb[rows, :]).astype(BF16)
            vbuf[rows, 0:128] = m[:, 256 * h + 128:256 * h + 256].astype(BF16)
            vbuf[rows, 128:256] = jnp.ones((128, 128), BF16)

    loop(0, 4, kv_build)

    def c_wg(j):
        yy = (yb + j) % 4
        return rc(wd4.at[yy, hr], wd4.at[yy, hr], wg_s.at[yy], wg_r.at[yy], sib, t)

    def c_wg_in(j):
        yy = (yb + j) % 4
        hs = pl.ds(mo(128 * (1 - core), 128), 128)
        return rc(wd4.at[yy, hs], wd4.at[yy, hs], wg_s.at[yy], wg_r.at[yy], sib, t)

    def wd_fwd(j):
        yy = (yb + j) % 4
        yr_in(wd4.at[yy, hr], wd4.at[yy, hr], wd_s, wd_r, j).wait_recv()
        c_wg(j).start()

    loop(1, 4, wd_fwd)

    def c_ctx(j):
        return yr(csend.at[(yb + j) % 4], ctx4.at[yb], ca_s, ca_r, j)

    def attn(j):
        i = (yb + 1 + j) % 4
        rows = pl.ds(mo(i * 256, 256), 256)
        k0 = mo(jnp.maximum(i - 2, 0) * 256, 256)
        keys = pl.ds(k0, 768)
        kw = kbuf[keys, :]
        vw = vbuf[keys, :]
        kidx = lax.broadcasted_iota(jnp.int32, (256, 768), 1) + k0
        qidx = lax.broadcasted_iota(jnp.int32, (256, 768), 0) + i * 256
        lo = startb[rows, 0:1].astype(jnp.int32)
        ok = (kidx <= qidx) & (kidx >= lo)
        for h in range(2):
            sc = dot(qbuf[h, rows, :], kw, ((1,), (1,)))
            p = jnp.where(ok, jnp.exp2(sc), 0.0).astype(BF16)
            o = dot(p, vw)
            csend[i, :, 128 * h:128 * h + 128] = (o[:, 0:128] / o[:, 128:256]).astype(BF16)

        @pl.when(j < 3)
        def _():
            c_ctx(j + 1).start()

    loop(0, 4, attn)
    ctx4[yb] = csend[yb]

    loop(1, 4, lambda j: c_wg_in(j).wait_recv())
    loop(1, 4, lambda j: yr_in(csend.at[(yb + j) % 4], ctx4.at[(yb + j) % 4], ca_s, ca_r, j).wait_recv())
    dpart = (
        (dot(ctx4[0], wd4[0]) + dot(ctx4[1], wd4[1])) + (dot(ctx4[2], wd4[2]) + dot(ctx4[3], wd4[3]))
    ).astype(BF16)
    for m in range(8):
        dsend[m] = dpart[32 * m:32 * m + 32, :]

    def rs_copy(j):
        m = (t8 + j) % 8
        return rc(dsend.at[m], drecv.at[t8], rs_s.at[m], rs_r.at[t8], d, 8 * yb + m)

    def rs_in(j):
        m = (t8 + j) % 8
        return rc(dsend.at[m], drecv.at[m], rs_s.at[m], rs_r.at[m], d, 8 * yb + m)

    loop(1, 8, lambda j: rs_copy(j).start())
    drecv[t8] = dsend[t8]

    loop(1, NT, lambda j: c_win_in((t + j) % NT).wait_recv())

    def wait_wout(jj):
        @pl.when(8 * b + jj != t)
        def _():
            c_wout_in(jj).wait_recv()

    loop(0, 8, wait_wout)
    fw1 = rc(win.at[core], win.at[core], wf_s.at[0], wf_r.at[0], sib, t)
    fw2 = rc(wout.at[core], wout.at[core], wf_s.at[1], wf_r.at[1], sib, t)
    fw1.start()
    fw2.start()

    def ctx_t(i):
        ctxt[i] = jnp.transpose(ctx4[i].astype(F32), (1, 0)).astype(BF16)

    loop(0, 4, ctx_t)
    loop(1, 4, lambda j: qd_in(dout, dout4.at[pl.ds(mo(32 * ((b + j) % 4), 32), 32)], do_s, do_r, j).wait_recv())
    fw1.wait_recv()
    fw2.wait_recv()
    dhid = dot(dout4[:, 0:512], wout[0], ((1,), (1,))) + dot(dout4[:, 512:1024], wout[1], ((1,), (1,)))

    loop(1, 8, lambda j: rs_in(j).wait_recv())
    down = lax.fori_loop(0, 8, lambda m, a: a + drecv[m].astype(F32), jnp.zeros((32, SIDE), F32))
    gate = jax.nn.sigmoid(glogit[...])
    prv = prev[...].astype(F32)
    mix = gate * down + (1.0 - gate) * prv
    r = lax.rsqrt(jnp.mean(mix * mix, axis=1, keepdims=True) + EPS)
    snorm4[own32, :] = (mix * r * sgain[...]).astype(BF16)
    loop(1, 4, lambda j: qd(snorm4.at[own32], snorm4.at[own32], sn_s, sn_r, j).start())

    def in32(j):
        return pl.ds(mo(32 * ((b + j) % 4), 32), 32)

    loop(1, 4, lambda j: qd_in(snorm4.at[in32(j)], snorm4.at[in32(j)], sn_s, sn_r, j).wait_recv())

    sn4 = snorm4[...]
    pre = jnp.concatenate([dot(sn4, win[0]), dot(sn4, win[1])], axis=1)
    sig_pre = jax.nn.sigmoid(pre)
    hid = (pre * sig_pre).astype(BF16)
    dpre = (dhid * sig_pre * (1.0 + pre * (1.0 - sig_pre))).astype(BF16)
    dnp = (dot(dpre[:, 0:256], win[0], ((1,), (1,))) + dot(dpre[:, 256:512], win[1], ((1,), (1,)))).astype(BF16)
    for bb in range(4):
        dns[bb] = dnp[32 * bb:32 * bb + 32, :]
    loop(1, 4, lambda j: qd(dns.at[(b + j) % 4], dnr.at[b], dn_s, dn_r, j).start())
    dnr[b] = dns[b]
    sop = jnp.concatenate([dot(hid, wout[0]), dot(hid, wout[1])], axis=1).astype(BF16)
    for bb in range(4):
        sos[bb] = sop[32 * bb:32 * bb + 32, :]
    loop(1, 4, lambda j: qd(sos.at[(b + j) % 4], sor.at[b], so_s, so_r, j).start())
    sor[b] = sos[b]
    gin_l = dot(sn4, dpre, ((0,), (0,))).astype(BF16)
    for dd in range(4):
        gsi[dd] = gin_l[:, 128 * dd:128 * dd + 128]
    gout_l = dot(hid, dout4[...], ((0,), (0,))).astype(BF16)
    for dd in range(4):
        gso[dd] = gout_l[:, 256 * dd:256 * dd + 256]

    loop(1, 4, lambda j: qd_in(dns.at[0], dnr.at[(b + j) % 4], dn_s, dn_r, j).wait_recv())
    dn = (dnr[0].astype(F32) + dnr[1].astype(F32)) + (dnr[2].astype(F32) + dnr[3].astype(F32))
    scaled = dn * sgain[...]
    dmix = (
        dout[...].astype(F32)
        + r * scaled
        - mix * (r * r * r) * jnp.mean(scaled * mix, axis=1, keepdims=True)
    )
    dd_rows = pl.ds(mo(32 * t8, 32), 32)
    ddall[dd_rows, :] = (dmix * gate).astype(BF16)

    def c_ag(j):
        m = (t8 + j) % 8
        return rc(ddall.at[dd_rows], ddall.at[dd_rows], ag_s.at[m], ag_r.at[t8], d, 8 * yb + m)

    def c_ag_in(j):
        m = (t8 + j) % 8
        return rc(ddall.at[dd_rows], ddall.at[pl.ds(mo(32 * m, 32), 32)], ag_s.at[m], ag_r.at[m], d, 8 * yb + m)

    loop(1, 8, lambda j: c_ag(j).start())
    o_dprev[...] = (dmix * (1.0 - gate)).astype(BF16)
    gv0[b, :, 0:SIDE] = jnp.sum(dn * mix * r, axis=0, keepdims=True)
    gv0[b, :, SIDE:] = gate * (1.0 - gate) * jnp.sum(dmix * (down - prv), axis=0, keepdims=True)
    loop(1, 4, lambda j: qd(gv0.at[b], gv0.at[b], v1_s, v1_r, j).start())

    def g1(xx, k):
        if k == 0:
            return rc(gsi.at[2 * xx + 1 - core], r1i.at[xx], g1_s.at[0, xx], g1_r.at[0, xx], sib, t)
        return rc(gso.at[2 * xx + 1 - core], r1o.at[xx], g1_s.at[1, xx], g1_r.at[1, xx], sib, t)

    for k in range(2):
        for xx in range(2):
            g1(xx, k).start()

    loop(1, 4, lambda j: qd_in(sos.at[0], sor.at[(b + j) % 4], so_s, so_r, j).wait_recv())
    o_side[...] = (
        mix + ((sor[0].astype(F32) + sor[1].astype(F32)) + (sor[2].astype(F32) + sor[3].astype(F32)))
    ).astype(BF16)

    loop(1, 4, lambda j: qd_in(gv0.at[0], gv0.at[(b + j) % 4], v1_s, v1_r, j).wait_recv())
    gv1[...] = (gv0[0] + gv0[1]) + (gv0[2] + gv0[3])
    cv2 = rc(gv1, gv2, v2_s, v2_r, sib, t)
    cv2.start()

    for xx in range(2):
        g1(xx, 0).wait_recv()
        a2i[xx] = (gsi[2 * xx + core].astype(F32) + r1i[xx].astype(F32)).astype(BF16)
    for xx in range(2):
        g1(xx, 1).wait_recv()
        a2o[xx] = (gso[2 * xx + core].astype(F32) + r1o[xx].astype(F32)).astype(BF16)
    cv2.wait_recv()
    me16 = xh * 8 + q
    gv3[me16] = gv1[...] + gv2[...]

    def peer(j):
        return (me16 + j) % 16

    def g2(p, src, k):
        xx = p // 8
        qq = p % 8
        dev = (2 * xx + core, 4 * qq + b)
        if k == 0:
            return rc(a2i.at[xx, pl.ds(mo(128 * qq, 128), 128)], r2i.at[src], g2i_s.at[p], g2i_r.at[src], *dev)
        if k == 1:
            return rc(a2o.at[xx, pl.ds(mo(64 * qq, 64), 64)], r2o.at[src], g2o_s.at[p], g2o_r.at[src], *dev)
        return rc(gv3.at[me16], gv3.at[src], v3_s.at[p], v3_r.at[src], *dev)

    for k in range(3):
        loop(1, 16, lambda j, k=k: g2(peer(j), me16, k).start())
    r2i[me16] = a2i[xh, pl.ds(mo(128 * q, 128), 128), :]
    r2o[me16] = a2o[xh, pl.ds(mo(64 * q, 64), 64), :]

    loop(1, 8, lambda j: c_ag_in(j).wait_recv())

    def gpart(yy):
        g = dot(ctxt[yy], ddall[...]).astype(BF16)
        for dd in range(4):
            gds[dd, yy] = g[64 * dd:64 * dd + 64, :]

    loop(0, 4, gpart)

    def h1(xx):
        return rc(gds.at[2 * xx + 1 - core], h1r.at[xx], h1_s.at[xx], h1_r.at[xx], sib, t)

    for xx in range(2):
        h1(xx).start()
    for xx in range(2):
        h1(xx).wait_recv()

        def h1_sum(yy, xx=xx):
            h2s[xx, yy] = (gds[2 * xx + core, yy].astype(F32) + h1r[xx, yy].astype(F32)).astype(BF16)

        loop(0, 4, h1_sum)
    me8 = xh * 4 + yb

    def h2(p, src):
        return rc(h2s.at[p // 4, p % 4], h2r.at[src], h2_s.at[p], h2_r.at[src], 2 * (p // 4) + core, 8 * (p % 4) + t8)

    loop(1, 8, lambda j: h2((me8 + j) % 8, me8).start())
    h2r[me8] = h2s[xh, yb]

    def dpc(src, dst, ss, rs, slot, j):
        dd = (d + j) % 4
        return rc(src, dst, ss.at[dd], rs.at[slot], dd, t)

    def q64(dd):
        return pl.ds(mo(64 * dd, 64), 64)

    for k in range(3):
        loop(1, 16, lambda j, k=k: g2(peer(j), peer(j), k).wait_recv())
    oi = lax.fori_loop(0, 16, lambda s, a: a + r2i[s].astype(F32), jnp.zeros((128, 128), F32))
    oo = lax.fori_loop(0, 16, lambda s, a: a + r2o[s].astype(F32), jnp.zeros((64, 256), F32))
    o3i[...] = oi.astype(BF16)
    o3o[...] = oo.astype(BF16)
    r3i[b] = o3i[own32, :]
    loop(1, 4, lambda j: qd(o3i.at[in32(j)], r3i.at[b], g3i_s, g3i_r, j).start())
    to_t = 8 * b + q
    from_t = 4 * wj + wb
    co3 = rc(o3o, r3o, g3o_s, g3o_r, d, to_t)

    @pl.when(to_t != t)
    def _():
        co3.start()

    @pl.when(to_t == t)
    def _():
        r3o[...] = o3o[...]

    o_gg[...] = lax.fori_loop(0, 16, lambda s, a: a + gv3[s], jnp.zeros((1, 2 * SIDE), F32))

    loop(1, 8, lambda j: h2((me8 + j) % 8, (me8 + j) % 8).wait_recv())
    gda[q64(d), :] = lax.fori_loop(
        0, 8, lambda m, a: a + h2r[m].astype(F32), jnp.zeros((64, SIDE), F32)
    ).astype(BF16)
    loop(1, 4, lambda j: dpc(gda.at[q64(d)], gda.at[q64(d)], da_s, da_r, d, j).start())

    loop(1, 4, lambda j: qd_in(o3i.at[own32], r3i.at[(b + j) % 4], g3i_s, g3i_r, j).wait_recv())

    @pl.when(from_t != t)
    def _():
        rc(o3o, r3o, g3o_s, g3o_r, d, from_t).wait_recv()

    r4i[d] = r3i[...]
    r4o[d] = r3o[...]
    loop(1, 4, lambda j: dpc(r4i.at[d], r4i.at[d], g4i_s, g4i_r, d, j).start())
    loop(1, 4, lambda j: dpc(r4o.at[d], r4o.at[d], g4o_s, g4o_r, d, j).start())

    loop(1, 4, lambda j: dpc(gda.at[q64(d)], gda.at[q64((d + j) % 4)], da_s, da_r, (d + j) % 4, j).wait_recv())
    o_gdown[...] = gda[...].astype(F32)
    loop(1, 4, lambda j: dpc(r4i.at[d], r4i.at[(d + j) % 4], g4i_s, g4i_r, (d + j) % 4, j).wait_recv())
    loop(1, 4, lambda j: dpc(r4o.at[d], r4o.at[(d + j) % 4], g4o_s, g4o_r, (d + j) % 4, j).wait_recv())
    for dd in range(4):
        for bb in range(4):
            o_gin[:, 512 * bb + 128 * dd:512 * bb + 128 * dd + 128] = r4i[dd, bb].astype(F32)
        o_gout[:, 256 * dd:256 * dd + 256] = r4o[dd].astype(F32)

    loop(1, NT, lambda j: c_win((t + j) % NT).wait_send())

    def wout_sent(j):
        qq = (q + j) % 8

        @pl.when(4 * qq + wb != t)
        def _():
            c_wout(qq).wait_send()

    loop(0, 8, wout_sent)
    fw1.wait_send()
    fw2.wait_send()
    loop(1, 4, lambda j: qd(dout, dout4.at[own32], do_s, do_r, j).wait_send())

    def kv_sent(i):
        prow = pl.ds(mo(i * 128, 128), 128)
        loop(1, 4, lambda j: rc(
            kvown.at[prow], kvrecv.at[b, prow], kv_s.at[i, (b + j) % 4], kv_r.at[i, b], d, 4 * q + (b + j) % 4
        ).wait_send())

    loop(0, 4, kv_sent)
    loop(1, 4, lambda j: c_wd(j).wait_send())
    loop(1, 4, lambda j: c_wg(j).wait_send())
    loop(1, 4, lambda j: c_ctx(j).wait_send())
    loop(1, 8, lambda j: rs_copy(j).wait_send())
    loop(1, 4, lambda j: qd(snorm4.at[own32], snorm4.at[own32], sn_s, sn_r, j).wait_send())
    loop(1, 4, lambda j: qd(dns.at[(b + j) % 4], dnr.at[b], dn_s, dn_r, j).wait_send())
    loop(1, 4, lambda j: qd(sos.at[(b + j) % 4], sor.at[b], so_s, so_r, j).wait_send())
    loop(1, 8, lambda j: c_ag(j).wait_send())
    loop(1, 4, lambda j: qd(gv0.at[b], gv0.at[b], v1_s, v1_r, j).wait_send())
    for k in range(2):
        for xx in range(2):
            g1(xx, k).wait_send()
    cv2.wait_send()
    for k in range(3):
        loop(1, 16, lambda j, k=k: g2(peer(j), me16, k).wait_send())
    for xx in range(2):
        h1(xx).wait_send()
    loop(1, 8, lambda j: h2((me8 + j) % 8, me8).wait_send())
    loop(1, 4, lambda j: qd(o3i.at[in32(j)], r3i.at[b], g3i_s, g3i_r, j).wait_send())

    @pl.when(to_t != t)
    def _():
        co3.wait_send()

    loop(1, 4, lambda j: dpc(gda.at[q64(d)], gda.at[q64(d)], da_s, da_r, d, j).wait_send())
    loop(1, 4, lambda j: dpc(r4i.at[d], r4i.at[d], g4i_s, g4i_r, d, j).wait_send())
    loop(1, 4, lambda j: dpc(r4o.at[d], r4o.at[d], g4o_s, g4o_r, d, j).wait_send())


def body(
    hidden_in, attn_gain, seg_ids, w_query, w_key, w_value, w_down,
    prev_side, gate_logit, side_gain, w_in, w_out, d_out,
):
    half = HD // 2
    fr = (10000.0 ** (-np.arange(half) * 2.0 / HD)).astype(np.float32)
    freq = jnp.asarray(np.concatenate([fr, fr])[None])
    win4 = jnp.pad(w_in.reshape(32, 32, 56), ((0, 0), (0, 0), (0, 8)))
    win4 = win4.reshape(32, 4, 2, 256).transpose(1, 2, 0, 3)
    woutp = jnp.pad(w_out, ((0, 8), (0, 0))).reshape(64, 2, 512).transpose(1, 0, 2)
    vm = pl.BlockSpec(memory_space=pltpu.VMEM)
    anym = pl.BlockSpec(memory_space=pl.ANY)
    dma = pltpu.SemaphoreType.DMA

    def V(shape, dt=BF16):
        return pltpu.VMEM(shape, dt)

    scratch = [
        V((T, D)), V((D, 256)), V((32, D)), V((32, D)), V((128, D)), V((4, 256, SIDE)),
        V((256, 128), F32), V((256, 256), F32), V((256, 128), F32), V((T, 128), F32), V((T, 128), F32), V((T, 128), F32),
        V((512, 128)), V((4, 512, 128)), V((2, T, 128)), V((T, 128)), V((T, 256)), V((4, 256, 256)), V((4, 256, 256)), V((4, 256, 256)),
        V((8, 32, SIDE)), V((8, 32, SIDE)),
        V((2, SIDE, 256)), V((2, 512, 512)), V((128, SIDE)), V((128, SIDE)),
        V((4, 32, SIDE)), V((4, 32, SIDE)), V((4, 32, SIDE)), V((4, 32, SIDE)),
        V((256, SIDE)), V((4, 4, 64, SIDE)), V((2, 4, 64, SIDE)), V((2, 4, 64, SIDE)), V((8, 64, SIDE)), V((256, SIDE)),
        V((4, SIDE, 128)), V((4, 512, 256)), V((2, SIDE, 128)), V((2, 512, 256)), V((2, SIDE, 128)), V((2, 512, 256)),
        V((16, 128, 128)), V((16, 64, 256)), V((128, 128)), V((64, 256)), V((4, 32, 128)), V((64, 256)),
        V((4, 4, 32, 128)), V((4, 64, 256)),
        V((4, 1, 2 * SIDE), F32), V((1, 2 * SIDE), F32), V((1, 2 * SIDE), F32), V((16, 1, 2 * SIDE), F32),
        dma((4,)), dma((4,)),
        dma((4, 4)), dma((4, 4)), dma((32,)), dma((32,)), dma((8,)), dma((8,)), dma((2,)), dma((2,)),
        dma((4,)), dma((4,)), dma((8,)), dma((8,)), dma((4,)), dma((4,)), dma((4,)), dma((4,)), dma((4,)), dma((4,)),
        dma((4,)), dma((4,)), dma((4,)), dma((4,)), dma((4,)), dma((4,)), dma((8,)), dma((8,)),
        dma((2,)), dma((2,)), dma((8,)), dma((8,)), dma((4,)), dma((4,)),
        dma((2, 2)), dma((2, 2)), dma((16,)), dma((16,)), dma((16,)), dma((16,)), dma((4,)), dma((4,)), dma, dma,
        dma((4,)), dma((4,)), dma((4,)), dma((4,)), dma((4,)), dma((4,)), dma, dma, dma((16,)), dma((16,)),
    ]
    out = pl.pallas_call(
        kernel,
        out_shape=(
            jax.ShapeDtypeStruct((32, SIDE), BF16),
            jax.ShapeDtypeStruct((32, SIDE), BF16),
            jax.ShapeDtypeStruct((256, SIDE), F32),
            jax.ShapeDtypeStruct((32, 2048), F32),
            jax.ShapeDtypeStruct((64, SIDE), F32),
            jax.ShapeDtypeStruct((1, 2 * SIDE), F32),
        ),
        in_specs=[anym] * 5 + [vm] * 9,
        out_specs=tuple([vm] * 6),
        scratch_shapes=scratch,
        compiler_params=pltpu.CompilerParams(
            collective_id=0, has_side_effects=True, vmem_limit_bytes=60 * 1024 * 1024
        ),
    )(
        hidden_in, w_query, w_key.T, w_value.T, w_down,
        attn_gain[None], seg_ids[None], freq, win4, woutp, prev_side, gate_logit[None], side_gain[None], d_out,
    )
    side_out, d_prev, g_down, gin, gout, gg = out
    g_in = gin.reshape(32, 32, 64)[:, :, :56].reshape(32, 1792)
    g_out = gout[:56]
    rank = lax.axis_index("tensor")
    g_gain = lax.dynamic_slice_in_dim(gg[0, :SIDE], rank * 32, 32, 0)
    g_gate = lax.dynamic_slice_in_dim(gg[0, SIDE:], rank * 32, 32, 0)
    return side_out, d_prev, g_down, g_in, g_out, g_gain, g_gate


def solution(mesh):
    return jax.shard_map(
        body,
        mesh=mesh,
        in_specs=(
            P("dp", None), P(), P("dp"), P(None, "tensor"), P(None, "tensor"), P(None, "tensor"),
            P("tensor", None), P(("dp", "tensor"), None), P(), P(), P("tensor", None), P("tensor", None),
            P(("dp", "tensor"), None),
        ),
        out_specs=(
            P(("dp", "tensor"), None), P(("dp", "tensor"), None), P("tensor", None), P("tensor", None),
            P("tensor", None), P("tensor"), P("tensor"),
        ),
        check_vma=False,
    )
```

```python
import jax
import jax.numpy as jnp
import numpy as np
from jax import lax
from jax.experimental import pallas as pl
from jax.experimental.pallas import tpu as pltpu
from jax.sharding import PartitionSpec as P

MESH = pl.DeviceIdType.MESH
F32 = jnp.float32
BF16 = jnp.bfloat16
D = 8192
HD = 128
T = 1024
NT = 32
NDP = 4
SIDE = 1024
EPS = 1e-5
QSCALE = 1.4426950408889634 / np.sqrt(128.0)


def dot(a, b, dims=((1,), (0,))):
    return lax.dot_general(a, b, (dims, ((), ())), preferred_element_type=F32)


def mo(x, n):
    return pl.multiple_of(x, n)


def loop(lo, hi, fn):
    def step(i, carry):
        fn(i)
        return carry

    lax.fori_loop(lo, hi, step, 0)


def sincos(a):
    n = jnp.floor(a * np.float32(2 / np.pi) + 0.5)
    r = a - n * np.float32(1.5703125)
    r = r - n * np.float32(4.837512969970703125e-4)
    r = r - n * np.float32(7.54978995489188216e-8)
    r2 = r * r
    s = r + r * r2 * (-1.6666654611e-1 + r2 * (8.3321608736e-3 - r2 * 1.9515295891e-4))
    c = 1.0 - 0.5 * r2 + r2 * r2 * (
        4.166664568298827e-2 + r2 * (-1.388731625493765e-3 + r2 * 2.443315711809948e-5)
    )
    m = n.astype(jnp.int32)
    odd = (m & 1) == 1
    sin = jnp.where(odd, c, s)
    cos = jnp.where(odd, s, c)
    sin = jnp.where((m & 2) == 2, -sin, sin)
    cos = jnp.where(((m + 1) & 2) == 2, -cos, cos)
    return sin, cos


def kernel(
    x_hbm, wq_hbm, wk_hbm, wv_hbm, wd_hbm,
    gain, seg, freq, w_in, w_out, prev, glogit, sgain, dout,
    o_side, o_dprev, o_gda, o_r4i, o_r4o, o_gg,
    win4, woutp, wout2,
    xbuf, wq, wk, wv, wkv, wd4, acc, accq, ssq, cosb, sinb, startb,
    kvown, kvrecv, qbuf, kbuf, vbuf, csend, ctx4, ctxt, dsend, drecv,
    win, wout, dout4, snorm4, dns, dnr, sos, sor, ddall, gds, h1r, h2s, h2r, gda,
    gsi, gso, r1i, r1o, a2i, a2o, r2i, r2o, o3i, o3o, r3i, r3o, r4i, r4o,
    gv0, gv1, gv2, gv3,
    lsem, xsem,
    kv_s, kv_r, wi_s, wi_r, wo_s, wo_r, wf_s, wf_r, do_s, do_r, rs_s, rs_r, wd_s, wd_r, wg_s, wg_r, ca_s, ca_r,
    sn_s, sn_r, dn_s, dn_r, so_s, so_r, ag_s, ag_r, h1_s, h1_r, h2_s, h2_r, da_s, da_r,
    g1_s, g1_r, g2i_s, g2i_r, g2o_s, g2o_r, g3i_s, g3i_r, g3o_s, g3o_r,
    g4i_s, g4i_r, g4o_s, g4o_r, v1_s, v1_r, v2_s, v2_r, v3_s, v3_r,
):
    d = lax.axis_index("dp")
    t = lax.axis_index("tensor")
    core = d % 2
    xh = d // 2
    q = t // 4
    b = t % 4
    yb = t // 8
    sib = xh * 2 + 1 - core

    def rc(src, dst, ss, rs, dd, tt):
        return pltpu.make_async_remote_copy(
            src_ref=src, dst_ref=dst, send_sem=ss, recv_sem=rs,
            device_id=(dd, tt), device_id_type=MESH,
        )

    ld_wk = pltpu.make_async_copy(wk_hbm, wk, lsem.at[0])
    ld_wv = pltpu.make_async_copy(wv_hbm, wv, lsem.at[1])
    ld_wq = pltpu.make_async_copy(wq_hbm, wq, lsem.at[2])
    ld_wd = pltpu.make_async_copy(wd_hbm, wd4.at[yb], lsem.at[3])
    ld_wd.start()
    ld_wk.start()
    ld_wv.start()

    def ldx(i):
        rows = pl.ds(mo(i * 256, 256), 256)
        return pltpu.make_async_copy(x_hbm.at[rows], xbuf.at[rows], xsem.at[i])

    ld_wq.start()
    ldx(0).start()

    bar = pltpu.get_barrier_semaphore()

    def sig(dd, tt):
        pl.semaphore_signal(bar, inc=1, device_id=(dd, tt), device_id_type=MESH)

    loop(1, NT, lambda j: sig(d, (t + j) % NT))
    sig(sib, t)
    sig((1 - xh) * 2 + 1 - core, t)
    loop(0, 8, lambda j: sig((1 - xh) * 2 + core, 4 * j + b))

    wif = w_in[...].astype(F32)
    wir = pltpu.roll(wif, 1792 - 64, 1)
    for bb in range(4):
        for h in range(2):
            c0 = 448 * bb + 256 * h
            win4[bb, h] = (wif[:, c0:c0 + 256] if bb % 2 == 0 else wir[:, c0 - 64:c0 + 192]).astype(BF16)
    wof = jnp.concatenate([w_out[...].astype(F32), jnp.zeros((8, SIDE), F32)], axis=0)
    for h in range(2):
        woutp[h] = wof[:, 512 * h:512 * h + 512].astype(BF16)

    ld_wd.wait()
    pl.semaphore_wait(bar, 41)

    t8 = t % 8
    hr = pl.ds(mo(128 * core, 128), 128)

    def yr(src, dst, ss, rs, j):
        yy = (yb + j) % 4
        return rc(src, dst, ss.at[yy], rs.at[yb], d, 8 * yy + t8)

    def yr_in(src, dst, ss, rs, j):
        yy = (yb + j) % 4
        return rc(src, dst, ss.at[yy], rs.at[yy], d, 8 * yy + t8)

    def c_wd(j):
        return yr(wd4.at[yb, hr], wd4.at[yb, hr], wd_s, wd_r, j)

    loop(1, 4, lambda j: c_wd(j).start())

    def c_win(tt):
        return rc(win4.at[tt % 4, core], win.at[core, pl.ds(mo(32 * t, 32), 32)], wi_s.at[tt], wi_r.at[t], d, tt)

    def c_win_in(ss):
        return rc(win4.at[0, core], win.at[core, pl.ds(mo(32 * ss, 32), 32)], wi_s.at[ss], wi_r.at[ss], d, ss)

    wb = t // 8
    wj = t % 8

    def c_wout(qq):
        return rc(woutp.at[core], wout.at[core, pl.ds(mo(64 * wj, 64), 64)], wo_s.at[qq], wo_r.at[wj], d, 4 * qq + wb)

    def c_wout_in(jj):
        return rc(woutp.at[core], wout.at[core, pl.ds(mo(64 * jj, 64), 64)], wo_s.at[jj], wo_r.at[jj], d, 8 * b + jj)

    def start_wout(j):
        qq = (q + j) % 8

        @pl.when(4 * qq + wb != t)
        def _():
            c_wout(qq).start()

    loop(0, 8, start_wout)

    @pl.when(wb == b)
    def _():
        wout[core, pl.ds(mo(64 * wj, 64), 64), :] = woutp[core]

    def qd(src, dst, ss, rs, j):
        bb = (b + j) % 4
        return rc(src, dst, ss.at[bb], rs.at[b], d, 4 * q + bb)

    def qd_in(src, dst, ss, rs, j):
        bb = (b + j) % 4
        return rc(src, dst, ss.at[bb], rs.at[bb], d, 4 * q + bb)

    own32 = pl.ds(mo(32 * b, 32), 32)
    loop(1, 4, lambda j: qd(dout, dout4.at[own32], do_s, do_r, j).start())
    dout4[own32, :] = dout[...]

    lane = lax.broadcasted_iota(jnp.int32, (1, 128), 1)
    segrow = seg[...].astype(F32)
    segcol = jnp.transpose(jnp.broadcast_to(segrow, (128, T)), (1, 0))
    cnt = jnp.zeros((T, 128), F32)
    for k in range(T // 128):
        cnt = cnt + jnp.where(segrow[:, 128 * k:128 * k + 128] < segcol, 1.0, 0.0)
    start = jnp.sum(cnt, axis=1, keepdims=True)
    tok = lax.broadcasted_iota(jnp.int32, (T, 128), 0).astype(F32)
    startb[...] = jnp.broadcast_to(start, (T, 128))
    sn, cs = sincos((tok - start) * freq[...])
    cosb[...] = cs
    sinb[...] = jnp.where(lane < 64, -sn, sn)

    ld_wk.wait()
    ld_wv.wait()
    gk = (wk[...].astype(F32) * gain[...]).astype(BF16)
    gvw = (wv[...].astype(F32) * gain[...]).astype(BF16)
    wkv[0:32, :] = gk
    wkv[32:64, :] = gvw
    wkv[64:96, :] = gk
    wkv[96:128, :] = gvw
    ld_wq.wait()

    def gain_q(i):
        rows = pl.ds(mo(i * 1024, 1024), 1024)
        gcol = jnp.transpose(jnp.broadcast_to(gain[:, rows], (128, 1024)), (1, 0))
        for h in range(2):
            hh = slice(128 * h, 128 * h + 128)
            wq[rows, hh] = (wq[rows, hh].astype(F32) * gcol).astype(BF16)

    ldx(1).start()
    loop(0, 8, gain_q)

    def kv_chunk(i):
        rows = pl.ds(mo(i * 256, 256), 256)
        ldx(i).wait()

        @pl.when(i < 2)
        def _():
            ldx(i + 2).start()

        acc[...] = jnp.zeros((256, 128), F32)
        accq[...] = jnp.zeros((256, 256), F32)
        ssq[...] = jnp.zeros((256, 128), F32)

        def kk(k):
            cols = pl.ds(mo(k * 2048, 2048), 2048)
            xb = xbuf[rows, cols]
            xf = xb.astype(F32)
            sq = xf * xf
            part = sq[:, 0:128]
            for m in range(1, 16):
                part = part + sq[:, 128 * m:128 * m + 128]
            ssq[...] = ssq[...] + part
            acc[...] = acc[...] + dot(xb, wkv[:, cols], ((1,), (1,)))
            accq[...] = accq[...] + dot(xb, wq[cols, :])

        loop(0, 4, kk)
        s = lax.rsqrt(jnp.sum(ssq[...], axis=1, keepdims=True) * (1.0 / D) + EPS)
        sb = jnp.broadcast_to(s, (256, 128))
        kv = acc[...] * sb
        piece = jnp.where(lane < 64, kv[0:128], kv[128:256]).astype(BF16)
        prow = pl.ds(mo(i * 128, 128), 128)
        kvown[prow, :] = piece
        kvrecv[b, prow, :] = piece
        loop(1, 4, lambda j: rc(
            kvown.at[prow], kvrecv.at[b, prow], kv_s.at[i, (b + j) % 4], kv_r.at[i, b], d, 4 * q + (b + j) % 4
        ).start())
        sb = sb * np.float32(QSCALE)
        co = cosb[rows, :] * sb
        si = sinb[rows, :] * sb
        for h in range(2):
            v = accq[:, 128 * h:128 * h + 128]
            qbuf[h, rows, :] = (v * co + pltpu.roll(v, 64, 1) * si).astype(BF16)

    loop(0, 4, kv_chunk)
    loop(1, NT, lambda j: c_win((t + j) % NT).start())
    win[core, pl.ds(mo(32 * t, 32), 32), :] = win4[b, core]

    def kv_in(i, j):
        bb = (b + j) % 4
        prow = pl.ds(mo(i * 128, 128), 128)
        rc(kvown.at[prow], kvrecv.at[bb, prow], kv_s.at[i, bb], kv_r.at[i, bb], d, 4 * q + bb).wait_recv()

    loop(0, 4, lambda i: loop(1, 4, lambda j: kv_in(i, j)))
    er = lax.broadcasted_iota(jnp.int32, (128, 512), 0)
    ec = lax.broadcasted_iota(jnp.int32, (128, 512), 1)
    base = ((er >> 6) << 8) + (((er >> 5) & 1) << 7) + (er & 31)

    def kv_build(i):
        prow = pl.ds(mo(i * 128, 128), 128)
        m = jnp.zeros((128, 512), F32)
        for bb in range(4):
            sel = jnp.where(ec == base + 32 * bb, 1.0, 0.0).astype(BF16)
            m = m + dot(kvrecv[bb, prow, :], sel)
        for h in range(2):
            rows = pl.ds(mo(i * 256 + h * 128, 128), 128)
            kf = m[:, 256 * h:256 * h + 128]
            kbuf[rows, :] = (kf * cosb[rows, :] + pltpu.roll(kf, 64, 1) * sinb[rows, :]).astype(BF16)
            vbuf[rows, 0:128] = m[:, 256 * h + 128:256 * h + 256].astype(BF16)
            vbuf[rows, 128:256] = jnp.ones((128, 128), BF16)

    loop(0, 4, kv_build)

    def c_wg(j):
        yy = (yb + j) % 4
        return rc(wd4.at[yy, hr], wd4.at[yy, hr], wg_s.at[yy], wg_r.at[yy], sib, t)

    def c_wg_in(j):
        yy = (yb + j) % 4
        hs = pl.ds(mo(128 * (1 - core), 128), 128)
        return rc(wd4.at[yy, hs], wd4.at[yy, hs], wg_s.at[yy], wg_r.at[yy], sib, t)

    def wd_fwd(j):
        yy = (yb + j) % 4
        yr_in(wd4.at[yy, hr], wd4.at[yy, hr], wd_s, wd_r, j).wait_recv()
        c_wg(j).start()

    loop(1, 4, wd_fwd)

    def c_ctx(j):
        return yr(csend.at[(yb + j) % 4], ctx4.at[yb], ca_s, ca_r, j)

    def attn(j):
        i = (yb + 1 + j) % 4
        rows = pl.ds(mo(i * 256, 256), 256)
        k0 = mo(jnp.maximum(i - 2, 0) * 256, 256)
        keys = pl.ds(k0, 768)
        kw = kbuf[keys, :]
        vw = vbuf[keys, :]
        kidx = lax.broadcasted_iota(jnp.int32, (256, 768), 1) + k0
        qidx = lax.broadcasted_iota(jnp.int32, (256, 768), 0) + i * 256
        lo = startb[rows, 0:1].astype(jnp.int32)
        ok = (kidx <= qidx) & (kidx >= lo)
        for h in range(2):
            sc = dot(qbuf[h, rows, :], kw, ((1,), (1,)))
            p = jnp.where(ok, jnp.exp2(sc), 0.0).astype(BF16)
            o = dot(p, vw)
            csend[i, :, 128 * h:128 * h + 128] = (o[:, 0:128] / o[:, 128:256]).astype(BF16)

        @pl.when(j < 3)
        def _():
            c_ctx(j + 1).start()

    loop(0, 4, attn)
    ctx4[yb] = csend[yb]

    loop(1, 4, lambda j: c_wg_in(j).wait_recv())
    loop(1, 4, lambda j: yr_in(csend.at[(yb + j) % 4], ctx4.at[(yb + j) % 4], ca_s, ca_r, j).wait_recv())
    dpart = (
        (dot(ctx4[0], wd4[0]) + dot(ctx4[1], wd4[1])) + (dot(ctx4[2], wd4[2]) + dot(ctx4[3], wd4[3]))
    ).astype(BF16)
    for m in range(8):
        dsend[m] = dpart[32 * m:32 * m + 32, :]

    def rs_copy(j):
        m = (t8 + j) % 8
        return rc(dsend.at[m], drecv.at[t8], rs_s.at[m], rs_r.at[t8], d, 8 * yb + m)

    def rs_in(j):
        m = (t8 + j) % 8
        return rc(dsend.at[m], drecv.at[m], rs_s.at[m], rs_r.at[m], d, 8 * yb + m)

    loop(1, 8, lambda j: rs_copy(j).start())
    drecv[t8] = dsend[t8]

    loop(1, NT, lambda j: c_win_in((t + j) % NT).wait_recv())

    def wait_wout(jj):
        @pl.when(8 * b + jj != t)
        def _():
            c_wout_in(jj).wait_recv()

    loop(0, 8, wait_wout)
    fw1 = rc(win.at[core], win.at[core], wf_s.at[0], wf_r.at[0], sib, t)
    fw2 = rc(wout.at[core], wout.at[core], wf_s.at[1], wf_r.at[1], sib, t)
    fw1.start()
    fw2.start()

    def ctx_t(i):
        ctxt[i] = jnp.transpose(ctx4[i].astype(F32), (1, 0)).astype(BF16)

    loop(0, 4, ctx_t)
    loop(1, 4, lambda j: qd_in(dout, dout4.at[pl.ds(mo(32 * ((b + j) % 4), 32), 32)], do_s, do_r, j).wait_recv())
    fw1.wait_recv()
    fw2.wait_recv()
    for h in range(2):
        wf = wout[h].astype(F32)
        wout2[h] = jnp.concatenate(
            [wf[64 * j:64 * j + 56] for j in range(8)] + [jnp.zeros((64, 512), F32)], axis=0
        ).astype(BF16)
    dhid = dot(dout4[:, 0:512], wout2[0], ((1,), (1,))) + dot(dout4[:, 512:1024], wout2[1], ((1,), (1,)))

    loop(1, 8, lambda j: rs_in(j).wait_recv())
    down = lax.fori_loop(0, 8, lambda m, a: a + drecv[m].astype(F32), jnp.zeros((32, SIDE), F32))
    gate = jax.nn.sigmoid(glogit[...])
    prv = prev[...].astype(F32)
    mix = gate * down + (1.0 - gate) * prv
    r = lax.rsqrt(jnp.mean(mix * mix, axis=1, keepdims=True) + EPS)
    snorm4[own32, :] = (mix * r * sgain[...]).astype(BF16)
    loop(1, 4, lambda j: qd(snorm4.at[own32], snorm4.at[own32], sn_s, sn_r, j).start())

    def in32(j):
        return pl.ds(mo(32 * ((b + j) % 4), 32), 32)

    loop(1, 4, lambda j: qd_in(snorm4.at[in32(j)], snorm4.at[in32(j)], sn_s, sn_r, j).wait_recv())

    sn4 = snorm4[...]
    pre = jnp.concatenate([dot(sn4, win[0]), dot(sn4, win[1])], axis=1)
    sig_pre = jax.nn.sigmoid(pre)
    hid = (pre * sig_pre).astype(BF16)
    dpre = (dhid * sig_pre * (1.0 + pre * (1.0 - sig_pre))).astype(BF16)
    dnp = (dot(dpre[:, 0:256], win[0], ((1,), (1,))) + dot(dpre[:, 256:512], win[1], ((1,), (1,)))).astype(BF16)
    for bb in range(4):
        dns[bb] = dnp[32 * bb:32 * bb + 32, :]
    loop(1, 4, lambda j: qd(dns.at[(b + j) % 4], dnr.at[b], dn_s, dn_r, j).start())
    dnr[b] = dns[b]
    sop = jnp.concatenate([dot(hid, wout2[0]), dot(hid, wout2[1])], axis=1).astype(BF16)
    for bb in range(4):
        sos[bb] = sop[32 * bb:32 * bb + 32, :]
    sor[b] = sos[b]
    gin_l = dot(sn4, dpre, ((0,), (0,))).astype(BF16)
    for dd in range(4):
        gsi[dd] = gin_l[:, 128 * dd:128 * dd + 128]
    gout_l = dot(hid, dout4[...], ((0,), (0,)))
    for dd in range(4):
        for j in range(8):
            gso[dd, 64 * j:64 * j + 64, :] = gout_l[56 * j:56 * j + 64, 256 * dd:256 * dd + 256].astype(BF16)

    def g1(xx, k):
        if k == 0:
            return rc(gsi.at[2 * xx + 1 - core], r1i.at[xx], g1_s.at[0, xx], g1_r.at[0, xx], sib, t)
        return rc(gso.at[2 * xx + 1 - core], r1o.at[xx], g1_s.at[1, xx], g1_r.at[1, xx], sib, t)

    for k in range(2):
        for xx in range(2):
            g1(xx, k).start()

    loop(1, 4, lambda j: qd_in(dns.at[0], dnr.at[(b + j) % 4], dn_s, dn_r, j).wait_recv())
    dn = (dnr[0].astype(F32) + dnr[1].astype(F32)) + (dnr[2].astype(F32) + dnr[3].astype(F32))
    scaled = dn * sgain[...]
    dmix = (
        dout[...].astype(F32)
        + r * scaled
        - mix * (r * r * r) * jnp.mean(scaled * mix, axis=1, keepdims=True)
    )
    dd_rows = pl.ds(mo(32 * t8, 32), 32)
    ddall[dd_rows, :] = (dmix * gate).astype(BF16)

    def c_ag(j):
        m = (t8 + j) % 8
        return rc(ddall.at[dd_rows], ddall.at[dd_rows], ag_s.at[m], ag_r.at[t8], d, 8 * yb + m)

    def c_ag_in(j):
        m = (t8 + j) % 8
        return rc(ddall.at[dd_rows], ddall.at[pl.ds(mo(32 * m, 32), 32)], ag_s.at[m], ag_r.at[m], d, 8 * yb + m)

    loop(1, 8, lambda j: c_ag(j).start())
    loop(1, 4, lambda j: qd(sos.at[(b + j) % 4], sor.at[b], so_s, so_r, j).start())
    o_dprev[...] = (dmix * (1.0 - gate)).astype(BF16)
    gv0[b, :, 0:SIDE] = jnp.sum(dn * mix * r, axis=0, keepdims=True)
    gv0[b, :, SIDE:] = gate * (1.0 - gate) * jnp.sum(dmix * (down - prv), axis=0, keepdims=True)
    loop(1, 4, lambda j: qd(gv0.at[b], gv0.at[b], v1_s, v1_r, j).start())

    loop(1, 4, lambda j: qd_in(gv0.at[0], gv0.at[(b + j) % 4], v1_s, v1_r, j).wait_recv())
    gv1[...] = (gv0[0] + gv0[1]) + (gv0[2] + gv0[3])
    cv2 = rc(gv1, gv2, v2_s, v2_r, sib, t)
    cv2.start()

    for xx in range(2):
        g1(xx, 0).wait_recv()
        a2i[xx] = (gsi[2 * xx + core].astype(F32) + r1i[xx].astype(F32)).astype(BF16)
    for xx in range(2):
        g1(xx, 1).wait_recv()
        a2o[xx] = (gso[2 * xx + core].astype(F32) + r1o[xx].astype(F32)).astype(BF16)
    cv2.wait_recv()
    me16 = xh * 8 + q
    gv3[me16] = gv1[...] + gv2[...]

    def peer(j):
        return (me16 + j) % 16

    def g2(p, src, k):
        xx = p // 8
        qq = p % 8
        dev = (2 * xx + core, 4 * qq + b)
        if k == 0:
            return rc(a2i.at[xx, pl.ds(mo(128 * qq, 128), 128)], r2i.at[src], g2i_s.at[p], g2i_r.at[src], *dev)
        if k == 1:
            return rc(a2o.at[xx, pl.ds(mo(64 * qq, 64), 64)], r2o.at[src], g2o_s.at[p], g2o_r.at[src], *dev)
        return rc(gv3.at[me16], gv3.at[src], v3_s.at[p], v3_r.at[src], *dev)

    for k in range(3):
        loop(1, 16, lambda j, k=k: g2(peer(j), me16, k).start())
    r2i[me16] = a2i[xh, pl.ds(mo(128 * q, 128), 128), :]
    r2o[me16] = a2o[xh, pl.ds(mo(64 * q, 64), 64), :]

    loop(1, 8, lambda j: c_ag_in(j).wait_recv())

    def gpart(yy):
        g = dot(ctxt[yy], ddall[...]).astype(BF16)
        for dd in range(4):
            gds[dd, yy] = g[64 * dd:64 * dd + 64, :]

    loop(0, 4, gpart)

    def h1(xx):
        return rc(gds.at[2 * xx + 1 - core], h1r.at[xx], h1_s.at[xx], h1_r.at[xx], sib, t)

    for xx in range(2):
        h1(xx).start()
    for xx in range(2):
        h1(xx).wait_recv()

        def h1_sum(yy, xx=xx):
            h2s[xx, yy] = (gds[2 * xx + core, yy].astype(F32) + h1r[xx, yy].astype(F32)).astype(BF16)

        loop(0, 4, h1_sum)
    me8 = xh * 4 + yb

    def h2(p, src):
        return rc(h2s.at[p // 4, p % 4], h2r.at[src], h2_s.at[p], h2_r.at[src], 2 * (p // 4) + core, 8 * (p % 4) + t8)

    loop(1, 8, lambda j: h2((me8 + j) % 8, me8).start())
    h2r[me8] = h2s[xh, yb]

    def dpc(src, dst, ss, rs, slot, j):
        dd = (d + j) % 4
        return rc(src, dst, ss.at[dd], rs.at[slot], dd, t)

    def q64(dd):
        return pl.ds(mo(64 * dd, 64), 64)

    loop(1, 4, lambda j: qd_in(sos.at[0], sor.at[(b + j) % 4], so_s, so_r, j).wait_recv())
    o_side[...] = (
        mix + ((sor[0].astype(F32) + sor[1].astype(F32)) + (sor[2].astype(F32) + sor[3].astype(F32)))
    ).astype(BF16)

    for k in range(3):
        loop(1, 16, lambda j, k=k: g2(peer(j), peer(j), k).wait_recv())
    oi = lax.fori_loop(0, 16, lambda s, a: a + r2i[s].astype(F32), jnp.zeros((128, 128), F32))
    oo = lax.fori_loop(0, 16, lambda s, a: a + r2o[s].astype(F32), jnp.zeros((64, 256), F32))
    o3i[...] = oi.astype(BF16)
    o3o[...] = oo.astype(BF16)
    r3i[b] = o3i[own32, :]
    loop(1, 4, lambda j: qd(o3i.at[in32(j)], r3i.at[b], g3i_s, g3i_r, j).start())
    to_t = 8 * b + q
    from_t = 4 * wj + wb
    co3 = rc(o3o, r3o, g3o_s, g3o_r, d, to_t)

    @pl.when(to_t != t)
    def _():
        co3.start()

    @pl.when(to_t == t)
    def _():
        r3o[...] = o3o[...]

    o_gg[...] = lax.fori_loop(0, 16, lambda s, a: a + gv3[s], jnp.zeros((1, 2 * SIDE), F32))

    loop(1, 8, lambda j: h2((me8 + j) % 8, (me8 + j) % 8).wait_recv())
    gda[q64(d), :] = lax.fori_loop(
        0, 8, lambda m, a: a + h2r[m].astype(F32), jnp.zeros((64, SIDE), F32)
    ).astype(BF16)
    loop(1, 4, lambda j: dpc(gda.at[q64(d)], gda.at[q64(d)], da_s, da_r, d, j).start())

    loop(1, 4, lambda j: qd_in(o3i.at[own32], r3i.at[(b + j) % 4], g3i_s, g3i_r, j).wait_recv())

    @pl.when(from_t != t)
    def _():
        rc(o3o, r3o, g3o_s, g3o_r, d, from_t).wait_recv()

    r4i[d] = r3i[...]
    r4o[d] = r3o[...]
    loop(1, 4, lambda j: dpc(r4i.at[d], r4i.at[d], g4i_s, g4i_r, d, j).start())
    loop(1, 4, lambda j: dpc(r4o.at[d], r4o.at[d], g4o_s, g4o_r, d, j).start())

    loop(1, 4, lambda j: dpc(gda.at[q64(d)], gda.at[q64((d + j) % 4)], da_s, da_r, (d + j) % 4, j).wait_recv())
    o_gda[...] = gda[...]
    loop(1, 4, lambda j: dpc(r4i.at[d], r4i.at[(d + j) % 4], g4i_s, g4i_r, (d + j) % 4, j).wait_recv())
    loop(1, 4, lambda j: dpc(r4o.at[d], r4o.at[(d + j) % 4], g4o_s, g4o_r, (d + j) % 4, j).wait_recv())
    o_r4i[...] = r4i[...]
    o_r4o[...] = r4o[...]

    loop(1, NT, lambda j: c_win((t + j) % NT).wait_send())

    def wout_sent(j):
        qq = (q + j) % 8

        @pl.when(4 * qq + wb != t)
        def _():
            c_wout(qq).wait_send()

    loop(0, 8, wout_sent)
    fw1.wait_send()
    fw2.wait_send()
    loop(1, 4, lambda j: qd(dout, dout4.at[own32], do_s, do_r, j).wait_send())

    def kv_sent(i):
        prow = pl.ds(mo(i * 128, 128), 128)
        loop(1, 4, lambda j: rc(
            kvown.at[prow], kvrecv.at[b, prow], kv_s.at[i, (b + j) % 4], kv_r.at[i, b], d, 4 * q + (b + j) % 4
        ).wait_send())

    loop(0, 4, kv_sent)
    loop(1, 4, lambda j: c_wd(j).wait_send())
    loop(1, 4, lambda j: c_wg(j).wait_send())
    loop(1, 4, lambda j: c_ctx(j).wait_send())
    loop(1, 8, lambda j: rs_copy(j).wait_send())
    loop(1, 4, lambda j: qd(snorm4.at[own32], snorm4.at[own32], sn_s, sn_r, j).wait_send())
    loop(1, 4, lambda j: qd(dns.at[(b + j) % 4], dnr.at[b], dn_s, dn_r, j).wait_send())
    loop(1, 4, lambda j: qd(sos.at[(b + j) % 4], sor.at[b], so_s, so_r, j).wait_send())
    loop(1, 8, lambda j: c_ag(j).wait_send())
    loop(1, 4, lambda j: qd(gv0.at[b], gv0.at[b], v1_s, v1_r, j).wait_send())
    for k in range(2):
        for xx in range(2):
            g1(xx, k).wait_send()
    cv2.wait_send()
    for k in range(3):
        loop(1, 16, lambda j, k=k: g2(peer(j), me16, k).wait_send())
    for xx in range(2):
        h1(xx).wait_send()
    loop(1, 8, lambda j: h2((me8 + j) % 8, me8).wait_send())
    loop(1, 4, lambda j: qd(o3i.at[in32(j)], r3i.at[b], g3i_s, g3i_r, j).wait_send())

    @pl.when(to_t != t)
    def _():
        co3.wait_send()

    loop(1, 4, lambda j: dpc(gda.at[q64(d)], gda.at[q64(d)], da_s, da_r, d, j).wait_send())
    loop(1, 4, lambda j: dpc(r4i.at[d], r4i.at[d], g4i_s, g4i_r, d, j).wait_send())
    loop(1, 4, lambda j: dpc(r4o.at[d], r4o.at[d], g4o_s, g4o_r, d, j).wait_send())


def finish(side, dprev, gda, gi, go, gg, o_side, o_dprev, o_gdown, o_gin, o_gout, o_gain, o_gate):
    o_side[...] = side[...]
    o_dprev[...] = dprev[...]
    o_gdown[...] = gda[...].astype(F32)
    cols = [None] * 14
    for bb in range(4):
        p = jnp.concatenate([gi[dd, bb].astype(F32) for dd in range(4)], axis=1)
        first = 7 * (bb // 2)
        if bb % 2 == 1:
            p = pltpu.roll(p, 64, 1)
            first += 3
        for m in range(4):
            v = p[:, 128 * m:128 * m + 128]
            cols[first + m] = v if cols[first + m] is None else cols[first + m] + v
    for m in range(14):
        o_gin[:, 128 * m:128 * m + 128] = cols[m]
    for dd in range(4):
        o_gout[:, 256 * dd:256 * dd + 256] = go[dd].astype(F32)[0:56]
    t = lax.axis_index("tensor")
    for k, o in enumerate((o_gain, o_gate)):
        x = gg[:, pl.ds(mo(k * SIDE + (t // 4) * 128, 128), 128)]
        v = x[:, 0:32]
        for m in range(1, 4):
            v = jnp.where(t % 4 == m, pltpu.roll(x, 128 - 32 * m, 1)[:, 0:32], v)
        o[...] = v


def body(
    hidden_in, attn_gain, seg_ids, w_query, w_key, w_value, w_down,
    prev_side, gate_logit, side_gain, w_in, w_out, d_out,
):
    half = HD // 2
    fr = (10000.0 ** (-np.arange(half) * 2.0 / HD)).astype(np.float32)
    freq = jnp.asarray(np.concatenate([fr, fr])[None])
    vm = pl.BlockSpec(memory_space=pltpu.VMEM)
    anym = pl.BlockSpec(memory_space=pl.ANY)
    dma = pltpu.SemaphoreType.DMA

    def V(shape, dt=BF16):
        return pltpu.VMEM(shape, dt)

    scratch = [
        V((4, 2, 32, 256)), V((2, 64, 512)), V((2, 512, 512)),
        V((T, D)), V((D, 256)), V((32, D)), V((32, D)), V((128, D)), V((4, 256, SIDE)),
        V((256, 128), F32), V((256, 256), F32), V((256, 128), F32), V((T, 128), F32), V((T, 128), F32), V((T, 128), F32),
        V((512, 128)), V((4, 512, 128)), V((2, T, 128)), V((T, 128)), V((T, 256)), V((4, 256, 256)), V((4, 256, 256)), V((4, 256, 256)),
        V((8, 32, SIDE)), V((8, 32, SIDE)),
        V((2, SIDE, 256)), V((2, 512, 512)), V((128, SIDE)), V((128, SIDE)),
        V((4, 32, SIDE)), V((4, 32, SIDE)), V((4, 32, SIDE)), V((4, 32, SIDE)),
        V((256, SIDE)), V((4, 4, 64, SIDE)), V((2, 4, 64, SIDE)), V((2, 4, 64, SIDE)), V((8, 64, SIDE)), V((256, SIDE)),
        V((4, SIDE, 128)), V((4, 512, 256)), V((2, SIDE, 128)), V((2, 512, 256)), V((2, SIDE, 128)), V((2, 512, 256)),
        V((16, 128, 128)), V((16, 64, 256)), V((128, 128)), V((64, 256)), V((4, 32, 128)), V((64, 256)),
        V((4, 4, 32, 128)), V((4, 64, 256)),
        V((4, 1, 2 * SIDE), F32), V((1, 2 * SIDE), F32), V((1, 2 * SIDE), F32), V((16, 1, 2 * SIDE), F32),
        dma((4,)), dma((4,)),
        dma((4, 4)), dma((4, 4)), dma((32,)), dma((32,)), dma((8,)), dma((8,)), dma((2,)), dma((2,)),
        dma((4,)), dma((4,)), dma((8,)), dma((8,)), dma((4,)), dma((4,)), dma((4,)), dma((4,)), dma((4,)), dma((4,)),
        dma((4,)), dma((4,)), dma((4,)), dma((4,)), dma((4,)), dma((4,)), dma((8,)), dma((8,)),
        dma((2,)), dma((2,)), dma((8,)), dma((8,)), dma((4,)), dma((4,)),
        dma((2, 2)), dma((2, 2)), dma((16,)), dma((16,)), dma((16,)), dma((16,)), dma((4,)), dma((4,)), dma, dma,
        dma((4,)), dma((4,)), dma((4,)), dma((4,)), dma((4,)), dma((4,)), dma, dma, dma((16,)), dma((16,)),
    ]
    out = pl.pallas_call(
        kernel,
        out_shape=(
            jax.ShapeDtypeStruct((32, SIDE), BF16),
            jax.ShapeDtypeStruct((32, SIDE), BF16),
            jax.ShapeDtypeStruct((256, SIDE), BF16),
            jax.ShapeDtypeStruct((4, 4, 32, 128), BF16),
            jax.ShapeDtypeStruct((4, 64, 256), BF16),
            jax.ShapeDtypeStruct((1, 2 * SIDE), F32),
        ),
        in_specs=[anym] * 5 + [vm] * 9,
        out_specs=tuple([vm] * 6),
        scratch_shapes=scratch,
        compiler_params=pltpu.CompilerParams(
            collective_id=0, has_side_effects=True, vmem_limit_bytes=60 * 1024 * 1024
        ),
    )(
        hidden_in, w_query, w_key.T, w_value.T, w_down,
        attn_gain[None], seg_ids[None], freq, w_in, w_out, prev_side, gate_logit[None], side_gain[None], d_out,
    )
    side_out, d_prev, g_down, g_in, g_out, g_gain, g_gate = pl.pallas_call(
        finish,
        out_shape=(
            jax.ShapeDtypeStruct((32, SIDE), BF16),
            jax.ShapeDtypeStruct((32, SIDE), BF16),
            jax.ShapeDtypeStruct((256, SIDE), F32),
            jax.ShapeDtypeStruct((32, 1792), F32),
            jax.ShapeDtypeStruct((56, SIDE), F32),
            jax.ShapeDtypeStruct((1, 32), F32),
            jax.ShapeDtypeStruct((1, 32), F32),
        ),
        in_specs=[vm] * 6,
        out_specs=tuple([vm] * 7),
    )(*out)
    return side_out, d_prev, g_down, g_in, g_out, g_gain.reshape(32), g_gate.reshape(32)


def solution(mesh):
    return jax.shard_map(
        body,
        mesh=mesh,
        in_specs=(
            P("dp", None), P(), P("dp"), P(None, "tensor"), P(None, "tensor"), P(None, "tensor"),
            P("tensor", None), P(("dp", "tensor"), None), P(), P(), P("tensor", None), P("tensor", None),
            P(("dp", "tensor"), None),
        ),
        out_specs=(
            P(("dp", "tensor"), None), P(("dp", "tensor"), None), P("tensor", None), P("tensor", None),
            P("tensor", None), P("tensor"), P("tensor"),
        ),
        check_vma=False,
    )
```

```python
import jax
import jax.numpy as jnp
import numpy as np
from jax import lax
from jax.experimental import pallas as pl
from jax.experimental.pallas import tpu as pltpu
from jax.sharding import PartitionSpec as P

MESH = pl.DeviceIdType.MESH
F32 = jnp.float32
BF16 = jnp.bfloat16
D = 8192
HD = 128
T = 1024
NT = 32
NDP = 4
SIDE = 1024
EPS = 1e-5
QSCALE = 1.4426950408889634 / np.sqrt(128.0)


def dot(a, b, dims=((1,), (0,))):
    return lax.dot_general(a, b, (dims, ((), ())), preferred_element_type=F32)


def mo(x, n):
    return pl.multiple_of(x, n)


def loop(lo, hi, fn):
    def step(i, carry):
        fn(i)
        return carry

    lax.fori_loop(lo, hi, step, 0)


def sincos(a):
    n = jnp.floor(a * np.float32(2 / np.pi) + 0.5)
    r = a - n * np.float32(1.5703125)
    r = r - n * np.float32(4.837512969970703125e-4)
    r = r - n * np.float32(7.54978995489188216e-8)
    r2 = r * r
    s = r + r * r2 * (-1.6666654611e-1 + r2 * (8.3321608736e-3 - r2 * 1.9515295891e-4))
    c = 1.0 - 0.5 * r2 + r2 * r2 * (
        4.166664568298827e-2 + r2 * (-1.388731625493765e-3 + r2 * 2.443315711809948e-5)
    )
    m = n.astype(jnp.int32)
    odd = (m & 1) == 1
    sin = jnp.where(odd, c, s)
    cos = jnp.where(odd, s, c)
    sin = jnp.where((m & 2) == 2, -sin, sin)
    cos = jnp.where(((m + 1) & 2) == 2, -cos, cos)
    return sin, cos


def kernel(
    x_hbm, wq_hbm, wk_hbm, wv_hbm, wd_hbm,
    gain, seg, freq, w_in, w_out, prev, glogit, sgain, dout,
    o_side, o_dprev, o_gda, o_r4i, o_r4o, o_gg,
    win4, woutp, wout2,
    xbuf, wq, wk, wv, wkv, wd4, acc, accq, ssq, cosb, sinb, startb,
    kvown, kvrecv, qbuf, kbuf, vbuf, csend, ctx4, ctxt, dsend, drecv,
    win, wout, dout4, snorm4, dns, dnr, sos, sor, ddall, gds, h1r, h2s, h2r, gda,
    gsi, gso, r1i, r1o, a2i, a2o, r2i, r2o, o3i, o3o, r3i, r3o, r4i, r4o,
    gv0, gv1, gv2, gv3,
    lsem, xsem,
    kv_s, kv_r, wi_s, wi_r, wo_s, wo_r, wf_s, wf_r, do_s, do_r, rs_s, rs_r, wd_s, wd_r, wg_s, wg_r, ca_s, ca_r,
    sn_s, sn_r, dn_s, dn_r, so_s, so_r, ag_s, ag_r, h1_s, h1_r, h2_s, h2_r, da_s, da_r,
    g1_s, g1_r, g2i_s, g2i_r, g2o_s, g2o_r, g3i_s, g3i_r, g3o_s, g3o_r,
    g4i_s, g4i_r, g4o_s, g4o_r, v1_s, v1_r, v2_s, v2_r, v3_s, v3_r,
):
    d = lax.axis_index("dp")
    t = lax.axis_index("tensor")
    core = d % 2
    xh = d // 2
    q = t // 4
    b = t % 4
    yb = t // 8
    sib = xh * 2 + 1 - core

    def rc(src, dst, ss, rs, dd, tt):
        return pltpu.make_async_remote_copy(
            src_ref=src, dst_ref=dst, send_sem=ss, recv_sem=rs,
            device_id=(dd, tt), device_id_type=MESH,
        )

    ld_wk = pltpu.make_async_copy(wk_hbm, wk, lsem.at[0])
    ld_wv = pltpu.make_async_copy(wv_hbm, wv, lsem.at[1])
    ld_wq = pltpu.make_async_copy(wq_hbm, wq, lsem.at[2])
    ld_wd = pltpu.make_async_copy(wd_hbm, wd4.at[yb], lsem.at[3])
    ld_wd.start()
    ld_wk.start()
    ld_wv.start()

    def ldx(i):
        rows = pl.ds(mo(i * 256, 256), 256)
        return pltpu.make_async_copy(x_hbm.at[rows], xbuf.at[rows], xsem.at[i])

    ld_wq.start()
    ldx(0).start()

    bar = pltpu.get_barrier_semaphore()

    def sig(dd, tt):
        pl.semaphore_signal(bar, inc=1, device_id=(dd, tt), device_id_type=MESH)

    loop(1, NT, lambda j: sig(d, (t + j) % NT))
    sig(sib, t)
    sig((1 - xh) * 2 + 1 - core, t)
    loop(0, 8, lambda j: sig((1 - xh) * 2 + core, 4 * j + b))

    wif = w_in[...].astype(F32)
    wir = pltpu.roll(wif, 1792 - 64, 1)
    for bb in range(4):
        for h in range(2):
            c0 = 448 * bb + 256 * h
            win4[bb, h] = (wif[:, c0:c0 + 256] if bb % 2 == 0 else wir[:, c0 - 64:c0 + 192]).astype(BF16)
    wof = jnp.concatenate([w_out[...].astype(F32), jnp.zeros((8, SIDE), F32)], axis=0)
    for h in range(2):
        woutp[h] = wof[:, 512 * h:512 * h + 512].astype(BF16)

    ld_wd.wait()
    pl.semaphore_wait(bar, 41)

    t8 = t % 8
    hr = pl.ds(mo(128 * core, 128), 128)

    def yr(src, dst, ss, rs, j):
        yy = (yb + j) % 4
        return rc(src, dst, ss.at[yy], rs.at[yb], d, 8 * yy + t8)

    def yr_in(src, dst, ss, rs, j):
        yy = (yb + j) % 4
        return rc(src, dst, ss.at[yy], rs.at[yy], d, 8 * yy + t8)

    def c_wd(j):
        return yr(wd4.at[yb, hr], wd4.at[yb, hr], wd_s, wd_r, j)

    loop(1, 4, lambda j: c_wd(j).start())

    def c_win(tt):
        return rc(win4.at[tt % 4, core], win.at[core, pl.ds(mo(32 * t, 32), 32)], wi_s.at[tt], wi_r.at[t], d, tt)

    def c_win_in(ss):
        return rc(win4.at[0, core], win.at[core, pl.ds(mo(32 * ss, 32), 32)], wi_s.at[ss], wi_r.at[ss], d, ss)

    wb = t // 8
    wj = t % 8

    def c_wout(qq):
        return rc(woutp.at[core], wout.at[core, pl.ds(mo(64 * wj, 64), 64)], wo_s.at[qq], wo_r.at[wj], d, 4 * qq + wb)

    def c_wout_in(jj):
        return rc(woutp.at[core], wout.at[core, pl.ds(mo(64 * jj, 64), 64)], wo_s.at[jj], wo_r.at[jj], d, 8 * b + jj)

    def start_wout(j):
        qq = (q + j) % 8

        @pl.when(4 * qq + wb != t)
        def _():
            c_wout(qq).start()

    loop(0, 8, start_wout)

    @pl.when(wb == b)
    def _():
        wout[core, pl.ds(mo(64 * wj, 64), 64), :] = woutp[core]

    def qd(src, dst, ss, rs, j):
        bb = (b + j) % 4
        return rc(src, dst, ss.at[bb], rs.at[b], d, 4 * q + bb)

    def qd_in(src, dst, ss, rs, j):
        bb = (b + j) % 4
        return rc(src, dst, ss.at[bb], rs.at[bb], d, 4 * q + bb)

    own32 = pl.ds(mo(32 * b, 32), 32)
    loop(1, 4, lambda j: qd(dout, dout4.at[own32], do_s, do_r, j).start())
    dout4[own32, :] = dout[...]

    lane = lax.broadcasted_iota(jnp.int32, (1, 128), 1)
    segrow = seg[...].astype(F32)
    segcol = jnp.transpose(jnp.broadcast_to(segrow, (128, T)), (1, 0))
    cnt = jnp.zeros((T, 128), F32)
    for k in range(T // 128):
        cnt = cnt + jnp.where(segrow[:, 128 * k:128 * k + 128] < segcol, 1.0, 0.0)
    start = jnp.sum(cnt, axis=1, keepdims=True)
    tok = lax.broadcasted_iota(jnp.int32, (T, 128), 0).astype(F32)
    startb[...] = jnp.broadcast_to(start, (T, 128))
    sn, cs = sincos((tok - start) * freq[...])
    cosb[...] = cs
    sinb[...] = jnp.where(lane < 64, -sn, sn)

    ld_wk.wait()
    ld_wv.wait()
    gk = (wk[...].astype(F32) * gain[...]).astype(BF16)
    gvw = (wv[...].astype(F32) * gain[...]).astype(BF16)
    wkv[0:32, :] = gk
    wkv[32:64, :] = gvw
    wkv[64:96, :] = gk
    wkv[96:128, :] = gvw
    ld_wq.wait()

    def gain_q(i):
        rows = pl.ds(mo(i * 1024, 1024), 1024)
        gcol = jnp.transpose(jnp.broadcast_to(gain[:, rows], (128, 1024)), (1, 0))
        for h in range(2):
            hh = slice(128 * h, 128 * h + 128)
            wq[rows, hh] = (wq[rows, hh].astype(F32) * gcol).astype(BF16)

    ldx(1).start()
    loop(0, 8, gain_q)

    def kv_chunk(i):
        rows = pl.ds(mo(i * 256, 256), 256)
        ldx(i).wait()

        @pl.when(i < 2)
        def _():
            ldx(i + 2).start()

        acc[...] = jnp.zeros((256, 128), F32)
        accq[...] = jnp.zeros((256, 256), F32)
        ssq[...] = jnp.zeros((256, 128), F32)

        def kk(k):
            cols = pl.ds(mo(k * 2048, 2048), 2048)
            xb = xbuf[rows, cols]
            xf = xb.astype(F32)
            sq = xf * xf
            part = sq[:, 0:128]
            for m in range(1, 16):
                part = part + sq[:, 128 * m:128 * m + 128]
            ssq[...] = ssq[...] + part
            acc[...] = acc[...] + dot(xb, wkv[:, cols], ((1,), (1,)))
            accq[...] = accq[...] + dot(xb, wq[cols, :])

        loop(0, 4, kk)
        s = lax.rsqrt(jnp.sum(ssq[...], axis=1, keepdims=True) * (1.0 / D) + EPS)
        sb = jnp.broadcast_to(s, (256, 128))
        kv = acc[...] * sb
        piece = jnp.where(lane < 64, kv[0:128], kv[128:256]).astype(BF16)
        prow = pl.ds(mo(i * 128, 128), 128)
        kvown[prow, :] = piece
        kvrecv[b, prow, :] = piece
        loop(1, 4, lambda j: rc(
            kvown.at[prow], kvrecv.at[b, prow], kv_s.at[i, (b + j) % 4], kv_r.at[i, b], d, 4 * q + (b + j) % 4
        ).start())
        sb = sb * np.float32(QSCALE)
        co = cosb[rows, :] * sb
        si = sinb[rows, :] * sb
        for h in range(2):
            v = accq[:, 128 * h:128 * h + 128]
            qbuf[h, rows, :] = (v * co + pltpu.roll(v, 64, 1) * si).astype(BF16)

    loop(0, 4, kv_chunk)
    loop(1, NT, lambda j: c_win((t + j) % NT).start())
    win[core, pl.ds(mo(32 * t, 32), 32), :] = win4[b, core]

    def kv_in(i, j):
        bb = (b + j) % 4
        prow = pl.ds(mo(i * 128, 128), 128)
        rc(kvown.at[prow], kvrecv.at[bb, prow], kv_s.at[i, bb], kv_r.at[i, bb], d, 4 * q + bb).wait_recv()

    loop(0, 4, lambda i: loop(1, 4, lambda j: kv_in(i, j)))
    er = lax.broadcasted_iota(jnp.int32, (128, 512), 0)
    ec = lax.broadcasted_iota(jnp.int32, (128, 512), 1)
    base = ((er >> 6) << 8) + (((er >> 5) & 1) << 7) + (er & 31)

    def kv_build(i):
        prow = pl.ds(mo(i * 128, 128), 128)
        m = jnp.zeros((128, 512), F32)
        for bb in range(4):
            sel = jnp.where(ec == base + 32 * bb, 1.0, 0.0).astype(BF16)
            m = m + dot(kvrecv[bb, prow, :], sel)
        for h in range(2):
            rows = pl.ds(mo(i * 256 + h * 128, 128), 128)
            kf = m[:, 256 * h:256 * h + 128]
            kbuf[rows, :] = (kf * cosb[rows, :] + pltpu.roll(kf, 64, 1) * sinb[rows, :]).astype(BF16)
            vbuf[rows, 0:128] = m[:, 256 * h + 128:256 * h + 256].astype(BF16)
            vbuf[rows, 128:256] = jnp.ones((128, 128), BF16)

    loop(0, 4, kv_build)

    def c_wg(j):
        yy = (yb + j) % 4
        return rc(wd4.at[yy, hr], wd4.at[yy, hr], wg_s.at[yy], wg_r.at[yy], sib, t)

    def c_wg_in(j):
        yy = (yb + j) % 4
        hs = pl.ds(mo(128 * (1 - core), 128), 128)
        return rc(wd4.at[yy, hs], wd4.at[yy, hs], wg_s.at[yy], wg_r.at[yy], sib, t)

    def wd_fwd(j):
        yy = (yb + j) % 4
        yr_in(wd4.at[yy, hr], wd4.at[yy, hr], wd_s, wd_r, j).wait_recv()
        c_wg(j).start()

    loop(1, 4, wd_fwd)

    def c_ctx(j):
        return yr(csend.at[(yb + j) % 4], ctx4.at[yb], ca_s, ca_r, j)

    def attn(j):
        i = (yb + 1 + j) % 4
        rows = pl.ds(mo(i * 256, 256), 256)
        k0 = mo(jnp.maximum(i - 2, 0) * 256, 256)
        keys = pl.ds(k0, 768)
        kw = kbuf[keys, :]
        vw = vbuf[keys, :]
        kidx = lax.broadcasted_iota(jnp.int32, (256, 768), 1) + k0
        qidx = lax.broadcasted_iota(jnp.int32, (256, 768), 0) + i * 256
        lo = startb[rows, 0:1].astype(jnp.int32)
        ok = (kidx <= qidx) & (kidx >= lo)
        for h in range(2):
            sc = dot(qbuf[h, rows, :], kw, ((1,), (1,)))
            p = jnp.where(ok, jnp.exp2(sc), 0.0).astype(BF16)
            o = dot(p, vw)
            csend[i, :, 128 * h:128 * h + 128] = (o[:, 0:128] / o[:, 128:256]).astype(BF16)

        @pl.when(j < 3)
        def _():
            c_ctx(j + 1).start()

    loop(0, 4, attn)
    ctx4[yb] = csend[yb]

    loop(1, 4, lambda j: c_wg_in(j).wait_recv())
    loop(1, 4, lambda j: yr_in(csend.at[(yb + j) % 4], ctx4.at[(yb + j) % 4], ca_s, ca_r, j).wait_recv())
    dpart = (
        (dot(ctx4[0], wd4[0]) + dot(ctx4[1], wd4[1])) + (dot(ctx4[2], wd4[2]) + dot(ctx4[3], wd4[3]))
    ).astype(BF16)
    for m in range(8):
        dsend[m] = dpart[32 * m:32 * m + 32, :]

    def rs_copy(j):
        m = (t8 + j) % 8
        return rc(dsend.at[m], drecv.at[t8], rs_s.at[m], rs_r.at[t8], d, 8 * yb + m)

    def rs_in(j):
        m = (t8 + j) % 8
        return rc(dsend.at[m], drecv.at[m], rs_s.at[m], rs_r.at[m], d, 8 * yb + m)

    loop(1, 8, lambda j: rs_copy(j).start())
    drecv[t8] = dsend[t8]

    loop(1, NT, lambda j: c_win_in((t + j) % NT).wait_recv())

    def wait_wout(jj):
        @pl.when(8 * b + jj != t)
        def _():
            c_wout_in(jj).wait_recv()

    loop(0, 8, wait_wout)
    fw1 = rc(win.at[core], win.at[core], wf_s.at[0], wf_r.at[0], sib, t)
    fw2 = rc(wout.at[core], wout.at[core], wf_s.at[1], wf_r.at[1], sib, t)
    fw1.start()
    fw2.start()

    def ctx_t(i):
        ctxt[i] = jnp.transpose(ctx4[i].astype(F32), (1, 0)).astype(BF16)

    loop(0, 4, ctx_t)
    loop(1, 4, lambda j: qd_in(dout, dout4.at[pl.ds(mo(32 * ((b + j) % 4), 32), 32)], do_s, do_r, j).wait_recv())
    fw1.wait_recv()
    fw2.wait_recv()
    for h in range(2):
        wf = wout[h].astype(F32)
        wout2[h] = jnp.concatenate(
            [wf[64 * j:64 * j + 56] for j in range(8)] + [jnp.zeros((64, 512), F32)], axis=0
        ).astype(BF16)
    dhid = dot(dout4[:, 0:512], wout2[0], ((1,), (1,))) + dot(dout4[:, 512:1024], wout2[1], ((1,), (1,)))

    loop(1, 8, lambda j: rs_in(j).wait_recv())
    down = lax.fori_loop(0, 8, lambda m, a: a + drecv[m].astype(F32), jnp.zeros((32, SIDE), F32))
    gate = jax.nn.sigmoid(glogit[...])
    prv = prev[...].astype(F32)
    mix = gate * down + (1.0 - gate) * prv
    r = lax.rsqrt(jnp.mean(mix * mix, axis=1, keepdims=True) + EPS)
    snorm4[own32, :] = (mix * r * sgain[...]).astype(BF16)
    loop(1, 4, lambda j: qd(snorm4.at[own32], snorm4.at[own32], sn_s, sn_r, j).start())

    def in32(j):
        return pl.ds(mo(32 * ((b + j) % 4), 32), 32)

    loop(1, 4, lambda j: qd_in(snorm4.at[in32(j)], snorm4.at[in32(j)], sn_s, sn_r, j).wait_recv())

    sn4 = snorm4[...]
    pre = jnp.concatenate([dot(sn4, win[0]), dot(sn4, win[1])], axis=1)
    sig_pre = jax.nn.sigmoid(pre)
    hid = (pre * sig_pre).astype(BF16)
    dpre = (dhid * sig_pre * (1.0 + pre * (1.0 - sig_pre))).astype(BF16)
    dnp = (dot(dpre[:, 0:256], win[0], ((1,), (1,))) + dot(dpre[:, 256:512], win[1], ((1,), (1,)))).astype(BF16)
    for bb in range(4):
        dns[bb] = dnp[32 * bb:32 * bb + 32, :]
    loop(1, 4, lambda j: qd(dns.at[(b + j) % 4], dnr.at[b], dn_s, dn_r, j).start())
    dnr[b] = dns[b]
    gin_l = dot(sn4, dpre, ((0,), (0,))).astype(BF16)
    for dd in range(4):
        gsi[dd] = gin_l[:, 128 * dd:128 * dd + 128]
    def g1(xx, k):
        if k == 0:
            return rc(gsi.at[2 * xx + 1 - core], r1i.at[xx], g1_s.at[0, xx], g1_r.at[0, xx], sib, t)
        return rc(gso.at[2 * xx + 1 - core], r1o.at[xx], g1_s.at[1, xx], g1_r.at[1, xx], sib, t)

    for xx in range(2):
        g1(xx, 0).start()

    loop(1, 4, lambda j: qd_in(dns.at[0], dnr.at[(b + j) % 4], dn_s, dn_r, j).wait_recv())
    dn = (dnr[0].astype(F32) + dnr[1].astype(F32)) + (dnr[2].astype(F32) + dnr[3].astype(F32))
    scaled = dn * sgain[...]
    dmix = (
        dout[...].astype(F32)
        + r * scaled
        - mix * (r * r * r) * jnp.mean(scaled * mix, axis=1, keepdims=True)
    )
    dd_rows = pl.ds(mo(32 * t8, 32), 32)
    ddall[dd_rows, :] = (dmix * gate).astype(BF16)

    def c_ag(j):
        m = (t8 + j) % 8
        return rc(ddall.at[dd_rows], ddall.at[dd_rows], ag_s.at[m], ag_r.at[t8], d, 8 * yb + m)

    def c_ag_in(j):
        m = (t8 + j) % 8
        return rc(ddall.at[dd_rows], ddall.at[pl.ds(mo(32 * m, 32), 32)], ag_s.at[m], ag_r.at[m], d, 8 * yb + m)

    loop(1, 8, lambda j: c_ag(j).start())

    gout_l = dot(hid, dout4[...], ((0,), (0,)))
    for dd in range(4):
        for j in range(8):
            gso[dd, 64 * j:64 * j + 64, :] = gout_l[56 * j:56 * j + 64, 256 * dd:256 * dd + 256].astype(BF16)

    for xx in range(2):
        g1(xx, 1).start()

    o_dprev[...] = (dmix * (1.0 - gate)).astype(BF16)
    gv0[b, :, 0:SIDE] = jnp.sum(dn * mix * r, axis=0, keepdims=True)
    gv0[b, :, SIDE:] = gate * (1.0 - gate) * jnp.sum(dmix * (down - prv), axis=0, keepdims=True)
    loop(1, 4, lambda j: qd(gv0.at[b], gv0.at[b], v1_s, v1_r, j).start())

    me16 = xh * 8 + q

    def peer(j):
        return (me16 + j) % 16

    def g2(p, src, k):
        xx = p // 8
        qq = p % 8
        dev = (2 * xx + core, 4 * qq + b)
        if k == 0:
            return rc(a2i.at[xx, pl.ds(mo(128 * qq, 128), 128)], r2i.at[src], g2i_s.at[p], g2i_r.at[src], *dev)
        if k == 1:
            return rc(a2o.at[xx, pl.ds(mo(64 * qq, 64), 64)], r2o.at[src], g2o_s.at[p], g2o_r.at[src], *dev)
        return rc(gv3.at[me16], gv3.at[src], v3_s.at[p], v3_r.at[src], *dev)

    for xx in range(2):
        g1(xx, 0).wait_recv()
        a2i[xx] = (gsi[2 * xx + core].astype(F32) + r1i[xx].astype(F32)).astype(BF16)
    loop(1, 16, lambda j: g2(peer(j), me16, 0).start())
    r2i[me16] = a2i[xh, pl.ds(mo(128 * q, 128), 128), :]
    for xx in range(2):
        g1(xx, 1).wait_recv()
        a2o[xx] = (gso[2 * xx + core].astype(F32) + r1o[xx].astype(F32)).astype(BF16)
    loop(1, 16, lambda j: g2(peer(j), me16, 1).start())
    r2o[me16] = a2o[xh, pl.ds(mo(64 * q, 64), 64), :]

    loop(1, 4, lambda j: qd_in(gv0.at[0], gv0.at[(b + j) % 4], v1_s, v1_r, j).wait_recv())
    gv1[...] = (gv0[0] + gv0[1]) + (gv0[2] + gv0[3])
    cv2 = rc(gv1, gv2, v2_s, v2_r, sib, t)
    cv2.start()

    loop(1, 8, lambda j: c_ag_in(j).wait_recv())

    def h1(xx, yy):
        return rc(gds.at[2 * xx + 1 - core, yy], h1r.at[xx, yy], h1_s.at[xx, yy], h1_r.at[xx, yy], sib, t)

    def gpart(j):
        yy = (yb + 1 + j) % 4
        g = dot(ctxt[yy], ddall[...]).astype(BF16)
        for dd in range(4):
            gds[dd, yy] = g[64 * dd:64 * dd + 64, :]
        for xx in range(2):
            h1(xx, yy).start()

    loop(0, 4, gpart)
    me8 = xh * 4 + yb

    def h2(p, src):
        return rc(h2s.at[p // 4, p % 4], h2r.at[src], h2_s.at[p], h2_r.at[src], 2 * (p // 4) + core, 8 * (p % 4) + t8)

    def h1_sum(j):
        yy = (yb + 1 + j) % 4
        for xx in range(2):
            h1(xx, yy).wait_recv()
            h2s[xx, yy] = (gds[2 * xx + core, yy].astype(F32) + h1r[xx, yy].astype(F32)).astype(BF16)

            @pl.when(xx * 4 + yy != me8)
            def _():
                h2(xx * 4 + yy, me8).start()

    loop(0, 4, h1_sum)
    h2r[me8] = h2s[xh, yb]
    cv2.wait_recv()
    gv3[me16] = gv1[...] + gv2[...]
    loop(1, 16, lambda j: g2(peer(j), me16, 2).start())
    sop = jnp.concatenate([dot(hid, wout2[0]), dot(hid, wout2[1])], axis=1).astype(BF16)
    for bb in range(4):
        sos[bb] = sop[32 * bb:32 * bb + 32, :]
    sor[b] = sos[b]
    loop(1, 4, lambda j: qd(sos.at[(b + j) % 4], sor.at[b], so_s, so_r, j).start())

    dx = 2 * (1 - xh) + core
    dy = 2 * (1 - xh) + 1 - core

    def over_dp(at, ss, rs):
        return dict(
            sib=rc(at(d), at(d), ss.at[0], rs.at[d], sib, t),
            x=rc(at(d), at(d), ss.at[1], rs.at[d], dx, t),
            fwd=rc(at(dx), at(dx), ss.at[2], rs.at[dx], sib, t),
            in_sib=rc(at(sib), at(sib), ss.at[0], rs.at[sib], sib, t),
            in_x=rc(at(dx), at(dx), ss.at[1], rs.at[dx], dx, t),
            in_fwd=rc(at(dy), at(dy), ss.at[2], rs.at[dy], sib, t),
        )

    def q64(dd):
        return pl.ds(mo(64 * dd, 64), 64)

    for k in range(2):
        loop(1, 16, lambda j, k=k: g2(peer(j), peer(j), k).wait_recv())
    oi = lax.fori_loop(0, 16, lambda s, a: a + r2i[s].astype(F32), jnp.zeros((128, 128), F32))
    oo = lax.fori_loop(0, 16, lambda s, a: a + r2o[s].astype(F32), jnp.zeros((64, 256), F32))
    o3i[...] = oi.astype(BF16)
    o3o[...] = oo.astype(BF16)
    r3i[b] = o3i[own32, :]
    loop(1, 4, lambda j: qd(o3i.at[in32(j)], r3i.at[b], g3i_s, g3i_r, j).start())
    to_t = 8 * b + q
    from_t = 4 * wj + wb
    co3 = rc(o3o, r3o, g3o_s, g3o_r, d, to_t)

    @pl.when(to_t != t)
    def _():
        co3.start()

    @pl.when(to_t == t)
    def _():
        r3o[...] = o3o[...]


    loop(1, 8, lambda j: h2((me8 + j) % 8, (me8 + j) % 8).wait_recv())
    gda[q64(d), :] = lax.fori_loop(
        0, 8, lambda m, a: a + h2r[m].astype(F32), jnp.zeros((64, SIDE), F32)
    ).astype(BF16)
    tda = over_dp(lambda p: gda.at[q64(p)], da_s, da_r)
    tda["x"].start()
    tda["sib"].start()

    loop(1, 4, lambda j: qd_in(o3i.at[own32], r3i.at[(b + j) % 4], g3i_s, g3i_r, j).wait_recv())

    @pl.when(from_t != t)
    def _():
        rc(o3o, r3o, g3o_s, g3o_r, d, from_t).wait_recv()

    r4i[d] = r3i[...]
    r4o[d] = r3o[...]
    t4i = over_dp(lambda p: r4i.at[p], g4i_s, g4i_r)
    t4o = over_dp(lambda p: r4o.at[p], g4o_s, g4o_r)
    for c in (t4i, t4o):
        c["x"].start()
        c["sib"].start()
    loop(1, 4, lambda j: qd_in(sos.at[0], sor.at[(b + j) % 4], so_s, so_r, j).wait_recv())
    o_side[...] = (
        mix + ((sor[0].astype(F32) + sor[1].astype(F32)) + (sor[2].astype(F32) + sor[3].astype(F32)))
    ).astype(BF16)
    loop(1, 16, lambda j: g2(peer(j), peer(j), 2).wait_recv())
    o_gg[...] = lax.fori_loop(0, 16, lambda s, a: a + gv3[s], jnp.zeros((1, 2 * SIDE), F32))
    for c in (tda, t4i, t4o):
        c["in_x"].wait_recv()
        c["fwd"].start()
    for c in (tda, t4i, t4o):
        c["in_sib"].wait_recv()
        c["in_fwd"].wait_recv()
    o_gda[...] = gda[...]
    o_r4i[...] = r4i[...]
    o_r4o[...] = r4o[...]

    loop(1, NT, lambda j: c_win((t + j) % NT).wait_send())

    def wout_sent(j):
        qq = (q + j) % 8

        @pl.when(4 * qq + wb != t)
        def _():
            c_wout(qq).wait_send()

    loop(0, 8, wout_sent)
    fw1.wait_send()
    fw2.wait_send()
    loop(1, 4, lambda j: qd(dout, dout4.at[own32], do_s, do_r, j).wait_send())

    def kv_sent(i):
        prow = pl.ds(mo(i * 128, 128), 128)
        loop(1, 4, lambda j: rc(
            kvown.at[prow], kvrecv.at[b, prow], kv_s.at[i, (b + j) % 4], kv_r.at[i, b], d, 4 * q + (b + j) % 4
        ).wait_send())

    loop(0, 4, kv_sent)
    loop(1, 4, lambda j: c_wd(j).wait_send())
    loop(1, 4, lambda j: c_wg(j).wait_send())
    loop(1, 4, lambda j: c_ctx(j).wait_send())
    loop(1, 8, lambda j: rs_copy(j).wait_send())
    loop(1, 4, lambda j: qd(snorm4.at[own32], snorm4.at[own32], sn_s, sn_r, j).wait_send())
    loop(1, 4, lambda j: qd(dns.at[(b + j) % 4], dnr.at[b], dn_s, dn_r, j).wait_send())
    loop(1, 4, lambda j: qd(sos.at[(b + j) % 4], sor.at[b], so_s, so_r, j).wait_send())
    loop(1, 8, lambda j: c_ag(j).wait_send())
    loop(1, 4, lambda j: qd(gv0.at[b], gv0.at[b], v1_s, v1_r, j).wait_send())
    for k in range(2):
        for xx in range(2):
            g1(xx, k).wait_send()
    cv2.wait_send()
    for k in range(3):
        loop(1, 16, lambda j, k=k: g2(peer(j), me16, k).wait_send())
    for xx in range(2):
        loop(0, 4, lambda yy, xx=xx: h1(xx, yy).wait_send())
    loop(1, 8, lambda j: h2((me8 + j) % 8, me8).wait_send())
    loop(1, 4, lambda j: qd(o3i.at[in32(j)], r3i.at[b], g3i_s, g3i_r, j).wait_send())

    @pl.when(to_t != t)
    def _():
        co3.wait_send()

    for c in (tda, t4i, t4o):
        c["x"].wait_send()
        c["sib"].wait_send()
        c["fwd"].wait_send()


def finish(side, dprev, gda, gi, go, gg, o_side, o_dprev, o_gdown, o_gin, o_gout, o_gain, o_gate):
    o_side[...] = side[...]
    o_dprev[...] = dprev[...]
    o_gdown[...] = gda[...].astype(F32)
    cols = [None] * 14
    for bb in range(4):
        p = jnp.concatenate([gi[dd, bb].astype(F32) for dd in range(4)], axis=1)
        first = 7 * (bb // 2)
        if bb % 2 == 1:
            p = pltpu.roll(p, 64, 1)
            first += 3
        for m in range(4):
            v = p[:, 128 * m:128 * m + 128]
            cols[first + m] = v if cols[first + m] is None else cols[first + m] + v
    for m in range(14):
        o_gin[:, 128 * m:128 * m + 128] = cols[m]
    for dd in range(4):
        o_gout[:, 256 * dd:256 * dd + 256] = go[dd].astype(F32)[0:56]
    t = lax.axis_index("tensor")
    for k, o in enumerate((o_gain, o_gate)):
        x = gg[:, pl.ds(mo(k * SIDE + (t // 4) * 128, 128), 128)]
        v = x[:, 0:32]
        for m in range(1, 4):
            v = jnp.where(t % 4 == m, pltpu.roll(x, 128 - 32 * m, 1)[:, 0:32], v)
        o[...] = v


def body(
    hidden_in, attn_gain, seg_ids, w_query, w_key, w_value, w_down,
    prev_side, gate_logit, side_gain, w_in, w_out, d_out,
):
    half = HD // 2
    fr = (10000.0 ** (-np.arange(half) * 2.0 / HD)).astype(np.float32)
    freq = jnp.asarray(np.concatenate([fr, fr])[None])
    vm = pl.BlockSpec(memory_space=pltpu.VMEM)
    anym = pl.BlockSpec(memory_space=pl.ANY)
    dma = pltpu.SemaphoreType.DMA

    def V(shape, dt=BF16):
        return pltpu.VMEM(shape, dt)

    scratch = [
        V((4, 2, 32, 256)), V((2, 64, 512)), V((2, 512, 512)),
        V((T, D)), V((D, 256)), V((32, D)), V((32, D)), V((128, D)), V((4, 256, SIDE)),
        V((256, 128), F32), V((256, 256), F32), V((256, 128), F32), V((T, 128), F32), V((T, 128), F32), V((T, 128), F32),
        V((512, 128)), V((4, 512, 128)), V((2, T, 128)), V((T, 128)), V((T, 256)), V((4, 256, 256)), V((4, 256, 256)), V((4, 256, 256)),
        V((8, 32, SIDE)), V((8, 32, SIDE)),
        V((2, SIDE, 256)), V((2, 512, 512)), V((128, SIDE)), V((128, SIDE)),
        V((4, 32, SIDE)), V((4, 32, SIDE)), V((4, 32, SIDE)), V((4, 32, SIDE)),
        V((256, SIDE)), V((4, 4, 64, SIDE)), V((2, 4, 64, SIDE)), V((2, 4, 64, SIDE)), V((8, 64, SIDE)), V((256, SIDE)),
        V((4, SIDE, 128)), V((4, 512, 256)), V((2, SIDE, 128)), V((2, 512, 256)), V((2, SIDE, 128)), V((2, 512, 256)),
        V((16, 128, 128)), V((16, 64, 256)), V((128, 128)), V((64, 256)), V((4, 32, 128)), V((64, 256)),
        V((4, 4, 32, 128)), V((4, 64, 256)),
        V((4, 1, 2 * SIDE), F32), V((1, 2 * SIDE), F32), V((1, 2 * SIDE), F32), V((16, 1, 2 * SIDE), F32),
        dma((4,)), dma((4,)),
        dma((4, 4)), dma((4, 4)), dma((32,)), dma((32,)), dma((8,)), dma((8,)), dma((2,)), dma((2,)),
        dma((4,)), dma((4,)), dma((8,)), dma((8,)), dma((4,)), dma((4,)), dma((4,)), dma((4,)), dma((4,)), dma((4,)),
        dma((4,)), dma((4,)), dma((4,)), dma((4,)), dma((4,)), dma((4,)), dma((8,)), dma((8,)),
        dma((2, 4)), dma((2, 4)), dma((8,)), dma((8,)), dma((4,)), dma((4,)),
        dma((2, 2)), dma((2, 2)), dma((16,)), dma((16,)), dma((16,)), dma((16,)), dma((4,)), dma((4,)), dma, dma,
        dma((4,)), dma((4,)), dma((4,)), dma((4,)), dma((4,)), dma((4,)), dma, dma, dma((16,)), dma((16,)),
    ]
    out = pl.pallas_call(
        kernel,
        out_shape=(
            jax.ShapeDtypeStruct((32, SIDE), BF16),
            jax.ShapeDtypeStruct((32, SIDE), BF16),
            jax.ShapeDtypeStruct((256, SIDE), BF16),
            jax.ShapeDtypeStruct((4, 4, 32, 128), BF16),
            jax.ShapeDtypeStruct((4, 64, 256), BF16),
            jax.ShapeDtypeStruct((1, 2 * SIDE), F32),
        ),
        in_specs=[anym] * 5 + [vm] * 9,
        out_specs=tuple([vm] * 6),
        scratch_shapes=scratch,
        compiler_params=pltpu.CompilerParams(
            collective_id=0, has_side_effects=True, vmem_limit_bytes=60 * 1024 * 1024
        ),
    )(
        hidden_in, w_query, w_key.T, w_value.T, w_down,
        attn_gain[None], seg_ids[None], freq, w_in, w_out, prev_side, gate_logit[None], side_gain[None], d_out,
    )
    side_out, d_prev, g_down, g_in, g_out, g_gain, g_gate = pl.pallas_call(
        finish,
        out_shape=(
            jax.ShapeDtypeStruct((32, SIDE), BF16),
            jax.ShapeDtypeStruct((32, SIDE), BF16),
            jax.ShapeDtypeStruct((256, SIDE), F32),
            jax.ShapeDtypeStruct((32, 1792), F32),
            jax.ShapeDtypeStruct((56, SIDE), F32),
            jax.ShapeDtypeStruct((1, 32), F32),
            jax.ShapeDtypeStruct((1, 32), F32),
        ),
        in_specs=[vm] * 6,
        out_specs=tuple([vm] * 7),
    )(*out)
    return side_out, d_prev, g_down, g_in, g_out, g_gain.reshape(32), g_gate.reshape(32)


def solution(mesh):
    return jax.shard_map(
        body,
        mesh=mesh,
        in_specs=(
            P("dp", None), P(), P("dp"), P(None, "tensor"), P(None, "tensor"), P(None, "tensor"),
            P("tensor", None), P(("dp", "tensor"), None), P(), P(), P("tensor", None), P("tensor", None),
            P(("dp", "tensor"), None),
        ),
        out_specs=(
            P(("dp", "tensor"), None), P(("dp", "tensor"), None), P("tensor", None), P("tensor", None),
            P("tensor", None), P("tensor"), P("tensor"),
        ),
        check_vma=False,
    )
```
